512 devices in a mesh: row: 64 (over x, z, core), col: 8 (over y).
Axes of the slice: x: 4, y: 8, z: 8, core: 2. Of those that a mesh axis runs over, the one named last changes fastest.
Arguments:
- features: bfloat16 [64, 65536], P(None, ('row', 'col')), may hold values from -6 to 6
- lengthscale: float32 [64], replicated, may hold values from 5 to 12
- right_side: float32 [16, 65536], P(None, ('row', 'col')), may hold values from -40 to 40
Outputs:
- solution: float32 [16, 65536], P(None, ('row', 'col'))
- residual: float32 [16, 65536], P(None, ('row', 'col'))
The draws below stay inside these ranges and needn't reach their ends.
All inputs are finite; a program needn't handle non-finite values.
Results may differ from the reference program's by a relative error of at most 0.0069.
Values may be sent and summed in bfloat16 or wider, within the bound.
No kernel may reach another device: no remote copies, remote signals or barrier semaphores. Data moves between devices by JAX's collectives and lax.ppermute only.
A program may use at most 64 MiB of HBM per device.

```python
import math
import jax
import jax.numpy as jnp
from jax import lax

F = 64
PROBES = 16
ITERS = 2
POINTS = 65536


def draw_features(key, part):
    key = jax.random.fold_in(key, 23)
    key_mix, key_latent, key_noise = jax.random.split(key, 3)
    mixing = jax.random.normal(key_mix, (F, 4), jnp.float32) * 0.91
    latent = jax.random.normal(key_latent, (4, POINTS), jnp.float32)
    noise = jax.random.normal(key_noise, (F, POINTS), jnp.float32) * 0.68
    mixed = noise
    for index in range(4):
        mixed = mixed + mixing[:, index:index + 1] * latent[index:index + 1, :]
    return jnp.clip(mixed, -6.0, 6.0).astype(jnp.bfloat16)


def draw_right_side(key, part):
    key = jax.random.fold_in(key, 11)
    first, second = jax.random.split(key)
    ramp = 1.0 + 2.0 * jnp.arange(POINTS, dtype=jnp.float32) / POINTS
    rough = jnp.exp(jax.random.uniform(second, (1, POINTS), jnp.float32) * jnp.log(10.0)) / 3.0
    base = jnp.clip(jax.random.normal(first, (PROBES, POINTS), jnp.float32), -4.0, 4.0)
    return base * ramp[None, :] * rough


def setup_inputs(seed: int = 0) -> dict:
    seeds = jax.random.split(jax.random.key(seed), 4)
    features = draw_features(jax.random.fold_in(seeds[3], 71), 0)
    lengthscale = jnp.clip(jnp.exp(jax.random.uniform(seeds[1], (F,), jnp.float32, math.log(5.0), math.log(12.0))), 5.0, 12.0)
    right_side = draw_right_side(jax.random.fold_in(seeds[3], 71), 0)
    return dict(features=features, lengthscale=lengthscale, right_side=right_side)


def reference(features, lengthscale, right_side):
    inverse = 1.0 / lengthscale
    scaled = (features.astype(jnp.float32) * inverse[:, None]).astype(jnp.bfloat16)
    wide = scaled.astype(jnp.float32)
    sqnorm = jnp.sum(wide * wide, axis=0)
    block = min(512, POINTS)
    nblocks = POINTS // block
    factor = float(POINTS) ** -0.5

    def apply(direction):
        packed = direction.astype(jnp.bfloat16).astype(jnp.float32)

        def one_block(index):
            start = (index * block).astype(jnp.int32)
            rows_z = lax.dynamic_slice_in_dim(wide, start, block, 1)
            rows_n = lax.dynamic_slice_in_dim(sqnorm, start, block, 0)
            inner = lax.dot_general(rows_z, wide, (((0,), (0,)), ((), ())), preferred_element_type=jnp.float32)
            tile = jnp.exp(-0.5 * (rows_n[:, None] + sqnorm[None, :] - 2.0 * inner)).astype(jnp.bfloat16)
            return lax.dot_general(packed, tile.astype(jnp.float32), (((1,), (1,)), ((), ())), preferred_element_type=jnp.float32)

        pieces = lax.map(one_block, jnp.arange(nblocks, dtype=jnp.int32))
        summed = jnp.transpose(pieces, (1, 0, 2)).reshape(direction.shape)
        return direction + factor * summed

    solution = jnp.zeros_like(right_side)
    residual = right_side
    direction = right_side
    norm_now = jnp.sum(residual * residual, axis=1, keepdims=True)
    for step in range(ITERS):
        image = apply(direction)
        alpha = norm_now / jnp.sum(direction * image, axis=1, keepdims=True)
        solution = solution + alpha * direction
        residual = residual - alpha * image
        norm_next = jnp.sum(residual * residual, axis=1, keepdims=True)
        direction = residual + (norm_next / norm_now) * direction
        norm_now = norm_next
    return solution, residual
```

```python
import functools

import jax
import jax.numpy as jnp
from jax import lax
from jax.experimental import pallas as pl
from jax.experimental.pallas import tpu as pltpu
from jax.sharding import Mesh, PartitionSpec as P

F32, BF16 = jnp.float32, jnp.bfloat16
EXTRA = 16
AXES = ("x", "z", "core", "y")
PARAMS = dict(vmem_limit_bytes=48 << 20)


def pieces(value):
    high = value.astype(BF16).astype(F32)
    middle = (value - high).astype(BF16).astype(F32)
    return high, middle, value - high - middle


def augmented(raw, inverse, offset):
    scaled = (raw.astype(F32) * inverse).astype(BF16)
    wide = scaled.astype(F32)
    half = jnp.sum(wide * wide, axis=0, keepdims=True) * -0.5
    high, middle, low = pieces(half)
    row = lax.broadcasted_iota(jnp.int32, (EXTRA, raw.shape[1]), 0)
    below = jnp.where(row < 6, 1.0, 0.0)
    for index, part in enumerate((high, middle, low)):
        below = jnp.where(row == offset + index, part, below)
    return jnp.concatenate([scaled, below.astype(BF16)], axis=0)


def first_product(feats, chunk, scale_ref, cols_ref, rows_ref, start_ref, tile_ref, sums_ref, cols, rows):
    inverse = 1.0 / scale_ref[...]
    ncols, width = cols_ref.shape[0], cols_ref.shape[2]

    @pl.when(pl.program_id(0) == 0)
    def _():
        for index in range(ncols):
            block = augmented(cols_ref[index], inverse, 0).astype(F32)
            cols[pl.ds(index * width, width), :] = jnp.transpose(block).astype(BF16)
        sums_ref[...] = start_ref[...]

    nrows = rows_ref.shape[0]
    for index in range(nrows):
        rows[:, index * width:(index + 1) * width] = augmented(rows_ref[index, :feats, :], inverse, 3)
    vectors = jnp.concatenate([rows_ref[index, feats:, :] for index in range(nrows)], axis=1)
    for begin in range(0, ncols * width, chunk):
        inner = jnp.dot(cols[begin:begin + chunk, :], rows[...], preferred_element_type=F32)
        tile = jnp.exp(inner).astype(BF16)
        tile_ref[begin:begin + chunk, :] = tile
        part = lax.dot_general(vectors, tile, (((1,), (1,)), ((), ())), preferred_element_type=F32)
        for index in range(chunk // width):
            sums_ref[begin // width + index] += part[:, index * width:(index + 1) * width]


def make_tile(scale, cols, rows, start, step=8, chunk=512):
    ncols, feats, width = cols.shape
    total, depth = rows.shape[0], feats + EXTRA
    probes = rows.shape[1] - feats
    whole = pl.BlockSpec((ncols, probes, width), lambda i: (0, 0, 0))
    return pl.pallas_call(
        functools.partial(first_product, feats, chunk),
        grid=(total // step,),
        in_specs=[
            pl.BlockSpec((feats, 1), lambda i: (0, 0)),
            pl.BlockSpec(cols.shape, lambda i: (0, 0, 0)),
            pl.BlockSpec((step,) + rows.shape[1:], lambda i: (i, 0, 0)),
            whole,
        ],
        out_specs=[pl.BlockSpec((ncols * width, step * width), lambda i: (0, i)), whole],
        out_shape=[
            jax.ShapeDtypeStruct((ncols * width, total * width), BF16),
            jax.ShapeDtypeStruct((ncols, probes, width), F32),
        ],
        scratch_shapes=[pltpu.VMEM((ncols * width, depth), BF16), pltpu.VMEM((depth, step * width), BF16)],
        compiler_params=pltpu.CompilerParams(**PARAMS),
    )(scale, cols, rows, start)


def second_product(tile_ref, rows_ref, start_ref, sums_ref):
    ncols, width = sums_ref.shape[0], sums_ref.shape[2]

    @pl.when(pl.program_id(0) == 0)
    def _():
        sums_ref[...] = start_ref[...]

    vectors = jnp.concatenate([rows_ref[index] for index in range(rows_ref.shape[0])], axis=1)
    part = lax.dot_general(vectors, tile_ref[...], (((1,), (1,)), ((), ())), preferred_element_type=F32)
    for index in range(ncols):
        sums_ref[index] += part[:, index * width:(index + 1) * width]


def use_tile(tile, rows, start, step=16):
    total, probes, width = rows.shape
    whole = pl.BlockSpec(start.shape, lambda i: (0, 0, 0))
    return pl.pallas_call(
        second_product,
        grid=(total // step,),
        in_specs=[
            pl.BlockSpec((tile.shape[0], step * width), lambda i: (0, i)),
            pl.BlockSpec((step, probes, width), lambda i: (i, 0, 0)),
            whole,
        ],
        out_specs=whole,
        out_shape=jax.ShapeDtypeStruct(start.shape, F32),
        compiler_params=pltpu.CompilerParams(**PARAMS),
    )(tile, rows, start)


def spread(factor, parts_ref, image_ref, copies_ref):
    image = jnp.sum(parts_ref[...], axis=0) * factor
    image_ref[...] = image
    small = image.astype(BF16)
    for index in range(copies_ref.shape[0]):
        copies_ref[index] = small


def moments(factor, parts_ref, right_ref, image_ref, second_ref, out_ref):
    right, image = right_ref[...], image_ref[...]
    second = jnp.sum(parts_ref[...], axis=0) * factor
    second_ref[...] = second
    lane = lax.broadcasted_iota(jnp.int32, right.shape, 1)
    row = lax.broadcasted_iota(jnp.int32, right.shape, 0)
    placed = jnp.zeros_like(right)
    pairs = ((right, right), (right, image), (image, image), (image, second), (right, second))
    for index, (left, other) in enumerate(pairs):
        value = jnp.sum(left * other, axis=1, keepdims=True)
        placed = jnp.where(lane == row + index * right.shape[0], value, placed)
    out_ref[...] = jnp.sum(placed, axis=0, keepdims=True)


def finish(all_ref, right_ref, image_ref, second_ref, solution_ref, residual_ref):
    right, image, second = right_ref[...], image_ref[...], second_ref[...]
    totals = jnp.sum(all_ref[...], axis=0, keepdims=True)
    lane = lax.broadcasted_iota(jnp.int32, right.shape, 1)
    row = lax.broadcasted_iota(jnp.int32, right.shape, 0)

    def moment(index):
        return jnp.sum(jnp.where(lane == row + index * right.shape[0], totals, 0.0), axis=1, keepdims=True)

    bb, bu, uu, uw, bw = [moment(index) for index in range(5)]
    curve = bb + bu
    alpha = bb / curve
    rest = bu / curve
    norm = rest * rest * bb - 2.0 * alpha * rest * bu + alpha * alpha * uu
    lead = rest + norm / bb
    bend = (
        lead * lead * bb - 2.0 * lead * alpha * bu + alpha * alpha * uu
        + lead * (lead * bu - alpha * uu) - alpha * (lead * bw - alpha * uw)
    )
    later = norm / bend
    direction = lead * right - alpha * image
    solution_ref[...] = alpha * right + later * direction
    residual_ref[...] = right - alpha * (right + image) - later * (direction + lead * image - alpha * second)


def per_device(features, lengthscale, right_side):
    nx, nz, ny = lax.axis_size("x"), lax.axis_size("z"), lax.axis_size("y")
    feats, width = features.shape
    probes = right_side.shape[0]
    total = width * nx * nz * ny * lax.axis_size("core")
    factor = float(total) ** (-0.5)
    block = jax.ShapeDtypeStruct(right_side.shape, F32)
    swap = [(0, 1), (1, 0)]

    def exchange(values, axes):
        return lax.all_to_all(values, axes, 0, 0, tiled=True)

    scale = lengthscale.reshape(feats, 1)
    packed = jnp.concatenate([features, right_side.astype(BF16)], axis=0)
    cols = exchange(jnp.broadcast_to(features, (ny, feats, width)), "y")
    near = exchange(jnp.broadcast_to(packed, (nx * nz, feats + probes, width)), ("x", "z"))
    far = lax.ppermute(near, "core", swap)
    zeros = jnp.zeros((ny, probes, width), F32)
    tile_near, sums = make_tile(scale, cols, near, zeros)
    tile_far, sums = make_tile(scale, cols, far, sums)

    image, copies = pl.pallas_call(
        functools.partial(spread, factor),
        out_shape=[block, jax.ShapeDtypeStruct((nx * nz, probes, width), BF16)],
    )(exchange(sums, "y"))
    near = exchange(copies, ("x", "z"))
    far = lax.ppermute(near, "core", swap)
    sums = use_tile(tile_far, far, use_tile(tile_near, near, zeros))

    second, local = pl.pallas_call(
        functools.partial(moments, factor),
        out_shape=[block, jax.ShapeDtypeStruct((1, width), F32)],
    )(exchange(sums, "y"), right_side, image)
    local = lax.psum(local, "core")
    everyone = exchange(jnp.broadcast_to(local, (nx * nz * ny, width)), ("x", "z", "y"))
    return pl.pallas_call(finish, out_shape=[block, block])(everyone, right_side, image, second)


def solution(mesh):
    fine = Mesh(mesh.devices.reshape(4, 8, 2, 8), AXES)
    placed = P(None, AXES)
    return jax.shard_map(
        per_device,
        mesh=fine,
        in_specs=(placed, P(), placed),
        out_specs=(placed, placed),
        check_vma=False,
    )
```

```python
import functools

import jax
import jax.numpy as jnp
from jax import lax
from jax.experimental import pallas as pl
from jax.experimental.pallas import tpu as pltpu
from jax.sharding import Mesh, PartitionSpec as P

F32, BF16 = jnp.float32, jnp.bfloat16
EXTRA = 16
PAD = 8
CHUNK = 256
AXES = ("x", "z", "core", "y")
VMEM = pl.BlockSpec(memory_space=pltpu.VMEM)


def call(kernel, *args, outs, limit=16, scratch=()):
    return pl.pallas_call(
        kernel,
        in_specs=[VMEM] * len(args),
        out_specs=jax.tree.map(lambda _: VMEM, outs),
        out_shape=outs,
        scratch_shapes=scratch,
        compiler_params=pltpu.CompilerParams(vmem_limit_bytes=limit << 20),
    )(*args)


def shaped(dtype, *shape):
    return jax.ShapeDtypeStruct(shape, dtype)


def pieces(value):
    high = value.astype(BF16).astype(F32)
    middle = (value - high).astype(BF16).astype(F32)
    return high, middle, value - high - middle


def augmented(raw, inverse, offset):
    scaled = (raw.astype(F32) * inverse).astype(BF16)
    wide = scaled.astype(F32)
    half = jnp.sum(wide * wide, axis=0, keepdims=True) * -0.5
    high, middle, low = pieces(half)
    row = lax.broadcasted_iota(jnp.int32, (EXTRA, raw.shape[1]), 0)
    below = jnp.where(row < 6, 1.0, 0.0)
    for index, part in enumerate((high, middle, low)):
        below = jnp.where(row == offset + index, part, below)
    return jnp.concatenate([scaled, below.astype(BF16)], axis=0)


def copies(features_ref, right_ref, cols_ref, rows_ref):
    features, right = features_ref[...], right_ref[...].astype(BF16)
    feats = features.shape[0]
    for index in range(cols_ref.shape[0]):
        cols_ref[index] = features
    for index in range(rows_ref.shape[0]):
        rows_ref[index, :feats, :] = features
        rows_ref[index, feats:, :] = right


def dot_last(left, right):
    return lax.dot_general(left, right, (((1,), (1,)), ((), ())), preferred_element_type=F32)


def first_product(scale_ref, cols_ref, near_ref, far_ref, tile_near_ref, tile_far_ref, out_ref, cols, rows, sums):
    inverse = 1.0 / scale_ref[...]
    ncols, feats, width = cols_ref.shape
    probes = near_ref.shape[1] - feats
    for index in range(ncols):
        block = augmented(cols_ref[index], inverse, 0).astype(F32)
        cols[index * width:(index + 1) * width, :] = jnp.transpose(block).astype(BF16)
    for turn, (rows_ref, tile_ref) in enumerate(((near_ref, tile_near_ref), (far_ref, tile_far_ref))):
        nrows = rows_ref.shape[0]
        for index in range(nrows):
            rows[:, index * width:(index + 1) * width] = augmented(rows_ref[index, :feats, :], inverse, 3)
        vectors = jnp.concatenate([rows_ref[index, feats:, :] for index in range(nrows)], axis=1)
        for begin in range(0, ncols * width, CHUNK):
            inner = jnp.dot(cols[begin:begin + CHUNK, :], rows[...], preferred_element_type=F32)
            tile = jnp.exp(inner).astype(BF16)
            tile_ref[begin:begin + CHUNK, :] = tile
            part = dot_last(vectors, tile)
            for index in range(CHUNK // width):
                place = begin // width + index
                piece = part[:, index * width:(index + 1) * width]
                sums[place] = piece if turn == 0 else sums[place] + piece
    for index in range(ncols):
        value = sums[index]
        high = value.astype(BF16)
        low = (value - high.astype(F32)).astype(BF16)
        for peer in range(ncols):
            out_ref[peer, index * probes:(index + 1) * probes, :] = high
        out_ref[index, ncols * probes:(ncols + 1) * probes, :] = high
        out_ref[index, (ncols + 1) * probes:, :] = low


def spread(factor, parts_ref, image_ref, out_ref):
    probes = image_ref.shape[0]
    begin = parts_ref.shape[1] - 2 * probes
    own = jnp.zeros(image_ref.shape, F32)
    for peer in range(parts_ref.shape[0]):
        own += parts_ref[peer, begin:begin + probes, :].astype(F32) + parts_ref[peer, begin + probes:, :].astype(F32)
    image = own * factor
    image_ref[...] = image
    small = image.astype(BF16)
    for index in range(out_ref.shape[0]):
        out_ref[index] = small


def placed(values, shape):
    lane = lax.broadcasted_iota(jnp.int32, shape, 1)
    row = lax.broadcasted_iota(jnp.int32, shape, 0)
    grid = jnp.zeros(shape, F32)
    for index, value in values:
        grid = jnp.where(lane == row + index * shape[0], value, grid)
    return jnp.sum(grid, axis=0, keepdims=True)


def column_images(factor, parts_ref, right_ref, image_ref, cols_ref, local_ref):
    probes = right_ref.shape[0]
    for index in range(cols_ref.shape[0]):
        total = jnp.zeros(right_ref.shape, F32)
        for peer in range(parts_ref.shape[0]):
            total += parts_ref[peer, index * probes:(index + 1) * probes, :].astype(F32)
        cols_ref[index] = total * factor
    right, image = right_ref[...], image_ref[...]
    pairs = ((right, right), (right, image), (image, image))
    sums = [(k, jnp.sum(a * b, axis=1, keepdims=True)) for k, (a, b) in enumerate(pairs)]
    local_ref[...] = placed(sums, right.shape)


def second_product(tile_ref, rows_ref, sums_ref):
    width = rows_ref.shape[2]
    vectors = jnp.concatenate([rows_ref[index] for index in range(rows_ref.shape[0])], axis=1)
    part = dot_last(vectors, tile_ref[...])
    for index in range(sums_ref.shape[0]):
        sums_ref[index] = part[:, index * width:(index + 1) * width]


def third_product(factor, tile_ref, rows_ref, start_ref, images_ref, local_ref, out_ref):
    ncols, probes, width = start_ref.shape
    vectors = jnp.concatenate([rows_ref[index] for index in range(rows_ref.shape[0])], axis=1)
    part = dot_last(vectors, tile_ref[...])
    total = jnp.zeros((probes, width), F32)
    for index in range(ncols):
        second = (start_ref[index] + part[:, index * width:(index + 1) * width]) * factor
        out_ref[index, :probes, :] = second
        total += second * images_ref[index]
    energy = placed([(3, jnp.sum(total, axis=1, keepdims=True))], (probes, width))
    row = lax.broadcasted_iota(jnp.int32, (PAD, width), 0)
    scalars = jnp.where(row == 0, energy + local_ref[...], 0.0)
    for index in range(ncols):
        out_ref[index, probes:, :] = scalars


def gathered(parts_ref, second_ref, out_ref):
    total = jnp.sum(parts_ref[...], axis=0)
    probes = second_ref.shape[0]
    second_ref[...] = total[:probes]
    out_ref[...] = jnp.broadcast_to(total[probes:probes + 1], out_ref.shape)


def finish(all_ref, right_ref, image_ref, second_ref, solution_ref, residual_ref):
    right, image, second = right_ref[...], image_ref[...], second_ref[...]
    totals = jnp.sum(all_ref[...], axis=0, keepdims=True)
    lane = lax.broadcasted_iota(jnp.int32, right.shape, 1)
    row = lax.broadcasted_iota(jnp.int32, right.shape, 0)

    def moment(index):
        return jnp.sum(jnp.where(lane == row + index * right.shape[0], totals, 0.0), axis=1, keepdims=True)

    bb, bu, uu, uw = [moment(index) for index in range(4)]
    curve = bb + bu
    alpha = bb / curve
    rest = bu / curve
    norm = rest * rest * bb - 2.0 * alpha * rest * bu + alpha * alpha * uu
    lead = rest + norm / bb
    bend = (
        lead * lead * bb - 2.0 * lead * alpha * bu + alpha * alpha * uu
        + lead * (lead * bu - alpha * uu) - alpha * (lead * uu - alpha * uw)
    )
    later = norm / bend
    direction = lead * right - alpha * image
    solution_ref[...] = alpha * right + later * direction
    residual_ref[...] = right - alpha * (right + image) - later * (direction + lead * image - alpha * second)


def per_device(features, lengthscale, right_side):
    nx, nz, ncore, ny = [lax.axis_size(axis) for axis in AXES]
    feats, width = features.shape
    probes = right_side.shape[0]
    plane = nx * nz
    factor = float(width * plane * ncore * ny) ** (-0.5)
    block = shaped(F32, probes, width)
    swap = [(0, 1), (1, 0)]

    def exchange(values, axes):
        return lax.all_to_all(values, axes, 0, 0, tiled=True)

    def held(array):
        return pltpu.with_memory_space_constraint(array, pltpu.VMEM)

    cols, rows = call(
        copies, features, right_side,
        outs=[shaped(BF16, ny, feats, width), shaped(BF16, plane, feats + probes, width)],
    )
    near = exchange(rows, ("x", "z"))
    far = lax.ppermute(near, "core", swap)
    cols = exchange(cols, "y")
    tile = pltpu.VMEM((ny * width, plane * width), BF16)
    tile_near, tile_far, parts = call(
        first_product, lengthscale.reshape(feats, 1), cols, near, far,
        outs=[tile, tile, shaped(BF16, ny, (ny + 2) * probes, width)],
        limit=24,
        scratch=[
            pltpu.VMEM((ny * width, feats + EXTRA), BF16),
            pltpu.VMEM((feats + EXTRA, plane * width), BF16),
            pltpu.VMEM((ny, probes, width), F32),
        ],
    )
    parts = exchange(parts, "y")
    image, rows = call(
        functools.partial(spread, factor), parts, outs=[block, shaped(BF16, plane, probes, width)]
    )
    near = exchange(rows, ("x", "z"))
    images, local = call(
        functools.partial(column_images, factor), parts, right_side, image,
        outs=[shaped(F32, ny, probes, width), shaped(F32, 1, width)],
    )
    far = lax.ppermute(near, "core", swap)
    sums = call(second_product, held(tile_near), near, outs=shaped(F32, ny, probes, width))
    sums = call(
        functools.partial(third_product, factor), held(tile_far), far, sums, images, local,
        outs=shaped(F32, ny, probes + PAD, width),
    )
    second, local = call(gathered, exchange(sums, "y"), outs=[block, shaped(F32, plane * ncore, width)])
    everyone = exchange(local, ("x", "z", "core"))
    return call(finish, everyone, right_side, image, second, outs=[block, block])


def solution(mesh):
    fine = Mesh(mesh.devices.reshape(4, 8, 2, 8), AXES)
    split = P(None, AXES)
    return jax.shard_map(
        per_device,
        mesh=fine,
        in_specs=(split, P(), split),
        out_specs=(split, split),
        check_vma=False,
    )
```

```python
import functools

import jax
import jax.numpy as jnp
from jax import lax
from jax.experimental import pallas as pl
from jax.experimental.pallas import tpu as pltpu
from jax.sharding import Mesh, PartitionSpec as P

F32, BF16 = jnp.float32, jnp.bfloat16
EXTRA = 16
PAD = 8
CHUNK = 256
AXES = ("x", "z", "core", "y")
VMEM = pl.BlockSpec(memory_space=pltpu.VMEM)


def call(kernel, *args, outs, limit=16, scratch=(), specs=None):
    return pl.pallas_call(
        kernel,
        in_specs=specs or [VMEM] * len(args),
        out_specs=jax.tree.map(lambda _: VMEM, outs),
        out_shape=outs,
        scratch_shapes=scratch,
        compiler_params=pltpu.CompilerParams(vmem_limit_bytes=limit << 20),
    )(*args)


def shaped(dtype, *shape):
    return jax.ShapeDtypeStruct(shape, dtype)


def pieces(value):
    high = value.astype(BF16).astype(F32)
    middle = (value - high).astype(BF16).astype(F32)
    return high, middle, value - high - middle


def augmented(raw, inverse, offset):
    scaled = (raw.astype(F32) * inverse).astype(BF16)
    wide = scaled.astype(F32)
    half = jnp.sum(wide * wide, axis=0, keepdims=True) * -0.5
    high, middle, low = pieces(half)
    row = lax.broadcasted_iota(jnp.int32, (EXTRA, raw.shape[1]), 0)
    below = jnp.where(row < 6, 1.0, 0.0)
    for index, part in enumerate((high, middle, low)):
        below = jnp.where(row == offset + index, part, below)
    return jnp.concatenate([scaled, below.astype(BF16)], axis=0)


def copies(features_ref, right_ref, rows_ref, kept_ref, held, sems):
    moves = [
        pltpu.make_async_copy(features_ref, held, sems.at[0]),
        pltpu.make_async_copy(right_ref, kept_ref, sems.at[1]),
    ]
    for move in moves:
        move.start()
    for move in moves:
        move.wait()
    features, right = held[...], kept_ref[...].astype(BF16)
    feats = features.shape[0]
    for index in range(rows_ref.shape[0]):
        rows_ref[index, :feats, :] = features
        rows_ref[index, feats:, :] = right


def columns(scale_ref, cols_ref, inverse_ref, out_ref):
    ncols, feats, width = cols_ref.shape
    lane = lax.broadcasted_iota(jnp.int32, (feats, feats), 1)
    row = lax.broadcasted_iota(jnp.int32, (feats, feats), 0)
    scale = jnp.sum(jnp.where(lane == row, scale_ref[...], 0.0), axis=1, keepdims=True)
    inverse = jnp.broadcast_to(1.0 / scale, (feats, width))
    inverse_ref[...] = inverse
    for index in range(ncols):
        block = augmented(cols_ref[index], inverse, 0).astype(F32)
        out_ref[index * width:(index + 1) * width, :] = jnp.transpose(block).astype(BF16)


def dot_last(left, right):
    return lax.dot_general(left, right, (((1,), (1,)), ((), ())), preferred_element_type=F32)


def tile_and_product(inverse_ref, cols_ref, rows_ref, tile_ref, rows, add):
    feats, width = inverse_ref.shape
    inverse = inverse_ref[...]
    nrows = rows_ref.shape[0]
    for index in range(nrows):
        rows[:, index * width:(index + 1) * width] = augmented(rows_ref[index, :feats, :], inverse, 3)
    vectors = jnp.concatenate([rows_ref[index, feats:, :] for index in range(nrows)], axis=1)
    for begin in range(0, cols_ref.shape[0], CHUNK):
        inner = jnp.dot(cols_ref[begin:begin + CHUNK, :], rows[...], preferred_element_type=F32)
        tile = jnp.exp(inner).astype(BF16)
        tile_ref[begin:begin + CHUNK, :] = tile
        part = dot_last(vectors, tile)
        for index in range(CHUNK // width):
            add(begin // width + index, part[:, index * width:(index + 1) * width])


def near_product(inverse_ref, cols_ref, rows_ref, tile_ref, sums_ref, rows):
    def add(index, piece):
        sums_ref[index] = piece

    tile_and_product(inverse_ref, cols_ref, rows_ref, tile_ref, rows, add)


def far_product(inverse_ref, cols_ref, rows_ref, sums_ref, tile_ref, out_ref, rows):
    ncols, probes, _ = sums_ref.shape

    def add(index, piece):
        value = sums_ref[index] + piece
        high = value.astype(BF16)
        for peer in range(ncols):
            out_ref[peer, index * probes:(index + 1) * probes, :] = high
        out_ref[index, ncols * probes:(ncols + 1) * probes, :] = high
        out_ref[index, (ncols + 1) * probes:, :] = (value - high.astype(F32)).astype(BF16)

    tile_and_product(inverse_ref, cols_ref, rows_ref, tile_ref, rows, add)


def spread(factor, parts_ref, image_ref, out_ref):
    probes = image_ref.shape[0]
    begin = parts_ref.shape[1] - 2 * probes
    own = jnp.zeros(image_ref.shape, F32)
    for peer in range(parts_ref.shape[0]):
        own += parts_ref[peer, begin:begin + probes, :].astype(F32) + parts_ref[peer, begin + probes:, :].astype(F32)
    image = own * factor
    image_ref[...] = image
    small = image.astype(BF16)
    for index in range(out_ref.shape[0]):
        out_ref[index] = small


def placed(values, shape):
    lane = lax.broadcasted_iota(jnp.int32, shape, 1)
    row = lax.broadcasted_iota(jnp.int32, shape, 0)
    grid = jnp.zeros(shape, F32)
    for index, value in values:
        grid = jnp.where(lane == row + index * shape[0], value, grid)
    return jnp.sum(grid, axis=0, keepdims=True)


def column_images(factor, parts_ref, right_ref, image_ref, cols_ref, local_ref):
    probes = right_ref.shape[0]
    for index in range(cols_ref.shape[0]):
        total = jnp.zeros(right_ref.shape, F32)
        for peer in range(parts_ref.shape[0]):
            total += parts_ref[peer, index * probes:(index + 1) * probes, :].astype(F32)
        cols_ref[index] = total * factor
    right, image = right_ref[...], image_ref[...]
    pairs = ((right, right), (right, image), (image, image))
    sums = [(k, jnp.sum(a * b, axis=1, keepdims=True)) for k, (a, b) in enumerate(pairs)]
    local_ref[...] = placed(sums, right.shape)


def second_product(tile_ref, rows_ref, sums_ref):
    width = rows_ref.shape[2]
    vectors = jnp.concatenate([rows_ref[index] for index in range(rows_ref.shape[0])], axis=1)
    part = dot_last(vectors, tile_ref[...])
    for index in range(sums_ref.shape[0]):
        sums_ref[index] = part[:, index * width:(index + 1) * width]


def third_product(factor, tile_ref, rows_ref, start_ref, images_ref, local_ref, out_ref):
    ncols, probes, width = start_ref.shape
    vectors = jnp.concatenate([rows_ref[index] for index in range(rows_ref.shape[0])], axis=1)
    part = dot_last(vectors, tile_ref[...])
    total = jnp.zeros((probes, width), F32)
    for index in range(ncols):
        second = (start_ref[index] + part[:, index * width:(index + 1) * width]) * factor
        out_ref[index, :probes, :] = second
        total += second * images_ref[index]
    energy = placed([(3, jnp.sum(total, axis=1, keepdims=True))], (probes, width))
    row = lax.broadcasted_iota(jnp.int32, (PAD, width), 0)
    scalars = jnp.where(row == 0, energy + local_ref[...], 0.0)
    for index in range(ncols):
        out_ref[index, probes:, :] = scalars


def gathered(parts_ref, second_ref, out_ref):
    total = jnp.sum(parts_ref[...], axis=0)
    probes = second_ref.shape[0]
    second_ref[...] = total[:probes]
    out_ref[...] = jnp.broadcast_to(total[probes:probes + 1], out_ref.shape)


def finish(all_ref, right_ref, image_ref, second_ref, solution_ref, residual_ref):
    right, image, second = right_ref[...], image_ref[...], second_ref[...]
    totals = jnp.sum(all_ref[...], axis=0, keepdims=True)
    lane = lax.broadcasted_iota(jnp.int32, right.shape, 1)
    row = lax.broadcasted_iota(jnp.int32, right.shape, 0)

    def moment(index):
        return jnp.sum(jnp.where(lane == row + index * right.shape[0], totals, 0.0), axis=1, keepdims=True)

    bb, bu, uu, uw = [moment(index) for index in range(4)]
    curve = bb + bu
    alpha = bb / curve
    rest = bu / curve
    norm = rest * rest * bb - 2.0 * alpha * rest * bu + alpha * alpha * uu
    lead = rest + norm / bb
    bend = (
        lead * lead * bb - 2.0 * lead * alpha * bu + alpha * alpha * uu
        + lead * (lead * bu - alpha * uu) - alpha * (lead * uu - alpha * uw)
    )
    later = norm / bend
    direction = lead * right - alpha * image
    solution_ref[...] = alpha * right + later * direction
    residual_ref[...] = right - alpha * (right + image) - later * (direction + lead * image - alpha * second)


def per_device(features, lengthscale, right_side):
    nx, nz, ncore, ny = [lax.axis_size(axis) for axis in AXES]
    feats, width = features.shape
    probes = right_side.shape[0]
    plane = nx * nz
    factor = float(width * plane * ncore * ny) ** (-0.5)
    block = shaped(F32, probes, width)
    swap = [(0, 1), (1, 0)]

    def exchange(values, axes):
        return lax.all_to_all(values, axes, 0, 0, tiled=True)

    def held(array):
        return pltpu.with_memory_space_constraint(array, pltpu.VMEM)

    rows, right = call(
        copies, features, right_side, specs=[pl.BlockSpec(memory_space=pltpu.HBM)] * 2,
        outs=[shaped(BF16, plane, feats + probes, width), pltpu.VMEM(block.shape, F32)],
        scratch=[pltpu.VMEM(features.shape, BF16), pltpu.SemaphoreType.DMA((2,))],
    )
    right = held(right)
    cols = lax.all_gather(features, "y")
    near = exchange(rows, ("x", "z"))
    inverse, cols = call(
        columns, lengthscale.reshape(1, feats), cols,
        outs=[shaped(F32, feats, width), shaped(BF16, ny * width, feats + EXTRA)],
    )
    near, inverse, cols = lax.optimization_barrier((near, inverse, cols))
    far = lax.ppermute(near, "core", swap)
    tile = pltpu.VMEM((ny * width, plane * width), BF16)
    scratch = [pltpu.VMEM((feats + EXTRA, plane * width), BF16)]
    tile_near, sums = call(
        near_product, inverse, cols, near, outs=[tile, shaped(F32, ny, probes, width)], limit=24, scratch=scratch
    )
    tile_far, parts = call(
        far_product, inverse, cols, far, sums, outs=[tile, shaped(BF16, ny, (ny + 2) * probes, width)],
        limit=24, scratch=scratch,
    )
    parts = exchange(parts, "y")
    image, rows = call(
        functools.partial(spread, factor), parts, outs=[block, shaped(BF16, plane, probes, width)]
    )
    near = exchange(rows, ("x", "z"))
    images, local = call(
        functools.partial(column_images, factor), parts, right, image,
        outs=[shaped(F32, ny, probes, width), shaped(F32, 1, width)],
    )
    near, images, local = lax.optimization_barrier((near, images, local))
    far = lax.ppermute(near, "core", swap)
    sums = call(second_product, held(tile_near), near, outs=shaped(F32, ny, probes, width))
    sums = call(
        functools.partial(third_product, factor), held(tile_far), far, sums, images, local,
        outs=shaped(F32, ny, probes + PAD, width),
    )
    second, local = call(gathered, exchange(sums, "y"), outs=[block, shaped(F32, plane * ncore, width)])
    everyone = exchange(local, ("x", "z", "core"))
    return call(finish, everyone, right, image, second, outs=[block, block])


def solution(mesh):
    fine = Mesh(mesh.devices.reshape(4, 8, 2, 8), AXES)
    split = P(None, AXES)
    return jax.shard_map(
        per_device,
        mesh=fine,
        in_specs=(split, P(), split),
        out_specs=(split, split),
        check_vma=False,
    )
```

```python
import functools

import jax
import jax.numpy as jnp
from jax import lax
from jax.experimental import pallas as pl
from jax.experimental.pallas import tpu as pltpu
from jax.sharding import Mesh, PartitionSpec as P

F32, BF16 = jnp.float32, jnp.bfloat16
EXTRA = 16
PAD = 8
CHUNK = 256
AXES = ("x", "z", "core", "y")
VMEM = pl.BlockSpec(memory_space=pltpu.VMEM)


def call(kernel, *args, outs, limit=16, scratch=(), specs=None):
    return pl.pallas_call(
        kernel,
        in_specs=specs or [VMEM] * len(args),
        out_specs=jax.tree.map(lambda _: VMEM, outs),
        out_shape=outs,
        scratch_shapes=scratch,
        compiler_params=pltpu.CompilerParams(vmem_limit_bytes=limit << 20),
    )(*args)


def shaped(dtype, *shape):
    return jax.ShapeDtypeStruct(shape, dtype)


def pieces(value):
    high = value.astype(BF16).astype(F32)
    middle = (value - high).astype(BF16).astype(F32)
    return high, middle, value - high - middle


def augmented(raw, inverse, offset):
    scaled = (raw.astype(F32) * inverse).astype(BF16)
    wide = scaled.astype(F32)
    half = jnp.sum(wide * wide, axis=0, keepdims=True) * -0.5
    high, middle, low = pieces(half)
    row = lax.broadcasted_iota(jnp.int32, (EXTRA, raw.shape[1]), 0)
    below = jnp.where(row < 6, 1.0, 0.0)
    for index, part in enumerate((high, middle, low)):
        below = jnp.where(row == offset + index, part, below)
    return jnp.concatenate([scaled, below.astype(BF16)], axis=0)


def copies(features_ref, right_ref, rows_ref, kept_ref, held, sems):
    moves = [
        pltpu.make_async_copy(features_ref, held, sems.at[0]),
        pltpu.make_async_copy(right_ref, kept_ref, sems.at[1]),
    ]
    for move in moves:
        move.start()
    for move in moves:
        move.wait()
    features, right = held[...], kept_ref[...].astype(BF16)
    feats = features.shape[0]
    for index in range(rows_ref.shape[0]):
        rows_ref[index, :feats, :] = features
        rows_ref[index, feats:, :] = right


def columns(scale_ref, cols_ref, inverse_ref, out_ref):
    ncols, feats, width = cols_ref.shape
    lane = lax.broadcasted_iota(jnp.int32, (feats, feats), 1)
    row = lax.broadcasted_iota(jnp.int32, (feats, feats), 0)
    scale = jnp.sum(jnp.where(lane == row, scale_ref[...], 0.0), axis=1, keepdims=True)
    inverse = jnp.broadcast_to(1.0 / scale, (feats, width))
    inverse_ref[...] = inverse
    for index in range(ncols):
        block = augmented(cols_ref[index], inverse, 0).astype(F32)
        out_ref[index * width:(index + 1) * width, :] = jnp.transpose(block).astype(BF16)


def dot_last(left, right):
    return lax.dot_general(left, right, (((1,), (1,)), ((), ())), preferred_element_type=F32)


def tile_and_product(inverse_ref, cols_ref, rows_ref, tile_ref, rows, add):
    feats, width = inverse_ref.shape
    inverse = inverse_ref[...]
    nrows = rows_ref.shape[0]
    for index in range(nrows):
        rows[:, index * width:(index + 1) * width] = augmented(rows_ref[index, :feats, :], inverse, 3)
    vectors = jnp.concatenate([rows_ref[index, feats:, :] for index in range(nrows)], axis=1)
    for begin in range(0, cols_ref.shape[0], CHUNK):
        inner = jnp.dot(cols_ref[begin:begin + CHUNK, :], rows[...], preferred_element_type=F32)
        tile = jnp.exp(inner).astype(BF16)
        tile_ref[begin:begin + CHUNK, :] = tile
        part = dot_last(vectors, tile)
        for index in range(CHUNK // width):
            add(begin // width + index, part[:, index * width:(index + 1) * width])


def near_product(inverse_ref, cols_ref, rows_ref, tile_ref, sums_ref, rows):
    def add(index, piece):
        sums_ref[index] = piece

    tile_and_product(inverse_ref, cols_ref, rows_ref, tile_ref, rows, add)


def far_product(inverse_ref, cols_ref, rows_ref, sums_ref, tile_ref, out_ref, rows):
    ncols, probes, _ = sums_ref.shape

    def add(index, piece):
        value = sums_ref[index] + piece
        high = value.astype(BF16)
        for peer in range(ncols):
            out_ref[peer, index * probes:(index + 1) * probes, :] = high
        out_ref[index, ncols * probes:(ncols + 1) * probes, :] = high
        out_ref[index, (ncols + 1) * probes:, :] = (value - high.astype(F32)).astype(BF16)

    tile_and_product(inverse_ref, cols_ref, rows_ref, tile_ref, rows, add)


def spread(factor, parts_ref, image_ref, out_ref):
    probes = image_ref.shape[0]
    begin = parts_ref.shape[1] - 2 * probes
    own = jnp.zeros(image_ref.shape, F32)
    for peer in range(parts_ref.shape[0]):
        own += parts_ref[peer, begin:begin + probes, :].astype(F32) + parts_ref[peer, begin + probes:, :].astype(F32)
    image = own * factor
    image_ref[...] = image
    small = image.astype(BF16)
    for index in range(out_ref.shape[0]):
        out_ref[index] = small


def placed(values, shape):
    lane = lax.broadcasted_iota(jnp.int32, shape, 1)
    row = lax.broadcasted_iota(jnp.int32, shape, 0)
    grid = jnp.zeros(shape, F32)
    for index, value in values:
        grid = jnp.where(lane == row + index * shape[0], value, grid)
    return jnp.sum(grid, axis=0, keepdims=True)


def column_images(factor, parts_ref, right_ref, image_ref, cols_ref, local_ref):
    probes = right_ref.shape[0]
    for index in range(cols_ref.shape[0]):
        total = jnp.zeros(right_ref.shape, F32)
        for peer in range(parts_ref.shape[0]):
            total += parts_ref[peer, index * probes:(index + 1) * probes, :].astype(F32)
        cols_ref[index] = total * factor
    right, image = right_ref[...], image_ref[...]
    pairs = ((right, right), (right, image), (image, image))
    sums = [(k, jnp.sum(a * b, axis=1, keepdims=True)) for k, (a, b) in enumerate(pairs)]
    local_ref[...] = placed(sums, right.shape)


def second_product(tile_ref, rows_ref, sums_ref):
    width = rows_ref.shape[2]
    vectors = jnp.concatenate([rows_ref[index] for index in range(rows_ref.shape[0])], axis=1)
    part = dot_last(vectors, tile_ref[...])
    for index in range(sums_ref.shape[0]):
        sums_ref[index] = part[:, index * width:(index + 1) * width]


def third_product(factor, tile_ref, rows_ref, start_ref, images_ref, local_ref, out_ref):
    ncols, probes, width = start_ref.shape
    vectors = jnp.concatenate([rows_ref[index] for index in range(rows_ref.shape[0])], axis=1)
    part = dot_last(vectors, tile_ref[...])
    total = jnp.zeros((probes, width), F32)
    for index in range(ncols):
        second = (start_ref[index] + part[:, index * width:(index + 1) * width]) * factor
        out_ref[index, :probes, :] = second
        total += second * images_ref[index]
    energy = placed([(3, jnp.sum(total, axis=1, keepdims=True))], (probes, width))
    row = lax.broadcasted_iota(jnp.int32, (PAD, width), 0)
    scalars = jnp.where(row == 0, energy + local_ref[...], 0.0)
    for index in range(ncols):
        out_ref[index, probes:, :] = scalars


def gathered(parts_ref, second_ref, out_ref):
    total = jnp.sum(parts_ref[...], axis=0)
    probes = second_ref.shape[0]
    second_ref[...] = total[:probes]
    out_ref[...] = jnp.broadcast_to(total[probes:probes + 1], out_ref.shape)


def finish(all_ref, right_ref, image_ref, second_ref, solution_ref, residual_ref):
    right, image, second = right_ref[...], image_ref[...], second_ref[...]
    totals = jnp.sum(all_ref[...], axis=0, keepdims=True)
    lane = lax.broadcasted_iota(jnp.int32, right.shape, 1)
    row = lax.broadcasted_iota(jnp.int32, right.shape, 0)

    def moment(index):
        return jnp.sum(jnp.where(lane == row + index * right.shape[0], totals, 0.0), axis=1, keepdims=True)

    bb, bu, uu, uw = [moment(index) for index in range(4)]
    curve = bb + bu
    alpha = bb / curve
    rest = bu / curve
    norm = rest * rest * bb - 2.0 * alpha * rest * bu + alpha * alpha * uu
    lead = rest + norm / bb
    bend = (
        lead * lead * bb - 2.0 * lead * alpha * bu + alpha * alpha * uu
        + lead * (lead * bu - alpha * uu) - alpha * (lead * uu - alpha * uw)
    )
    later = norm / bend
    direction = lead * right - alpha * image
    solution_ref[...] = alpha * right + later * direction
    residual_ref[...] = right - alpha * (right + image) - later * (direction + lead * image - alpha * second)


def per_device(features, lengthscale, right_side):
    nx, nz, ncore, ny = [lax.axis_size(axis) for axis in AXES]
    feats, width = features.shape
    probes = right_side.shape[0]
    plane = nx * nz
    factor = float(width * plane * ncore * ny) ** (-0.5)
    block = shaped(F32, probes, width)
    swap = [(0, 1), (1, 0)]

    def exchange(values, axes):
        return lax.all_to_all(values, axes, 0, 0, tiled=True)

    def held(array):
        return pltpu.with_memory_space_constraint(array, pltpu.VMEM)

    rows, right = call(
        copies, *[pltpu.with_memory_space_constraint(array, pltpu.HBM) for array in (features, right_side)], specs=[pl.BlockSpec(memory_space=pltpu.HBM)] * 2,
        outs=[pltpu.VMEM((plane, feats + probes, width), BF16), pltpu.VMEM(block.shape, F32)],
        scratch=[pltpu.VMEM(features.shape, BF16), pltpu.SemaphoreType.DMA((2,))],
    )
    right = held(right)
    cols = lax.all_gather(features, "y")
    near = exchange(rows, ("x", "z"))
    inverse, cols = call(
        columns, lengthscale.reshape(1, feats), cols,
        outs=[shaped(F32, feats, width), shaped(BF16, ny * width, feats + EXTRA)],
    )
    near, inverse, cols = lax.optimization_barrier((near, inverse, cols))
    far = lax.ppermute(near, "core", swap)
    tile = pltpu.VMEM((ny * width, plane * width), BF16)
    scratch = [pltpu.VMEM((feats + EXTRA, plane * width), BF16)]
    tile_near, sums = call(
        near_product, inverse, cols, near, outs=[tile, shaped(F32, ny, probes, width)], limit=24, scratch=scratch
    )
    tile_far, parts = call(
        far_product, inverse, cols, far, sums, outs=[tile, shaped(BF16, ny, (ny + 2) * probes, width)],
        limit=24, scratch=scratch,
    )
    parts = exchange(parts, "y")
    image, rows = call(
        functools.partial(spread, factor), parts, outs=[block, shaped(BF16, plane, probes, width)]
    )
    near = exchange(rows, ("x", "z"))
    images, local = call(
        functools.partial(column_images, factor), parts, right, image,
        outs=[shaped(F32, ny, probes, width), shaped(F32, 1, width)],
    )
    far = lax.ppermute(near, "core", swap)
    sums = call(second_product, held(tile_near), near, outs=shaped(F32, ny, probes, width))
    sums = call(
        functools.partial(third_product, factor), held(tile_far), far, sums, images, local,
        outs=shaped(F32, ny, probes + PAD, width),
    )
    second, local = call(gathered, exchange(sums, "y"), outs=[block, shaped(F32, plane * ncore, width)])
    everyone = exchange(local, ("x", "z", "core"))
    return call(finish, everyone, right, image, second, outs=[block, block])


def solution(mesh):
    fine = Mesh(mesh.devices.reshape(4, 8, 2, 8), AXES)
    split = P(None, AXES)
    return jax.shard_map(
        per_device,
        mesh=fine,
        in_specs=(split, P(), split),
        out_specs=(split, split),
        check_vma=False,
    )
```

```python
import functools

import jax
import jax.numpy as jnp
from jax import lax
from jax.experimental import pallas as pl
from jax.experimental.pallas import tpu as pltpu
from jax.sharding import Mesh, PartitionSpec as P

F32, BF16 = jnp.float32, jnp.bfloat16
EXTRA = 16
PAD = 8
CHUNK = 256
AXES = ("x", "z", "core", "y")
VMEM = pl.BlockSpec(memory_space=pltpu.VMEM)


def call(kernel, *args, outs, limit=16, scratch=(), specs=None):
    return pl.pallas_call(
        kernel,
        in_specs=specs or [VMEM] * len(args),
        out_specs=jax.tree.map(lambda _: VMEM, outs),
        out_shape=outs,
        scratch_shapes=scratch,
        compiler_params=pltpu.CompilerParams(vmem_limit_bytes=limit << 20),
    )(*args)


def shaped(dtype, *shape):
    return jax.ShapeDtypeStruct(shape, dtype)


def pieces(value):
    high = value.astype(BF16).astype(F32)
    middle = (value - high).astype(BF16).astype(F32)
    return high, middle, value - high - middle


def augmented(raw, inverse, offset):
    scaled = (raw.astype(F32) * inverse).astype(BF16)
    wide = scaled.astype(F32)
    half = jnp.sum(wide * wide, axis=0, keepdims=True) * -0.5
    high, middle, low = pieces(half)
    row = lax.broadcasted_iota(jnp.int32, (EXTRA, raw.shape[1]), 0)
    below = jnp.where(row < 6, 1.0, 0.0)
    for index, part in enumerate((high, middle, low)):
        below = jnp.where(row == offset + index, part, below)
    return jnp.concatenate([scaled, below.astype(BF16)], axis=0)


def copies(features_ref, right_ref, cols_ref, rows_ref, kept_ref, held, sems):
    moves = [
        pltpu.make_async_copy(features_ref, held, sems.at[0]),
        pltpu.make_async_copy(right_ref, kept_ref, sems.at[1]),
    ]
    for move in moves:
        move.start()
    for move in moves:
        move.wait()
    features, right = held[...], kept_ref[...].astype(BF16)
    feats = features.shape[0]
    for index in range(cols_ref.shape[0]):
        cols_ref[index] = features
    for index in range(rows_ref.shape[0]):
        rows_ref[index, :feats, :] = features
        rows_ref[index, feats:, :] = right


def columns(scale_ref, cols_ref, inverse_ref, out_ref):
    ncols, feats, width = cols_ref.shape
    lane = lax.broadcasted_iota(jnp.int32, (feats, feats), 1)
    row = lax.broadcasted_iota(jnp.int32, (feats, feats), 0)
    scale = jnp.sum(jnp.where(lane == row, scale_ref[...], 0.0), axis=1, keepdims=True)
    inverse = jnp.broadcast_to(1.0 / scale, (feats, width))
    inverse_ref[...] = inverse
    for index in range(ncols):
        block = augmented(cols_ref[index], inverse, 0).astype(F32)
        out_ref[index * width:(index + 1) * width, :] = jnp.transpose(block).astype(BF16)


def dot_last(left, right):
    return lax.dot_general(left, right, (((1,), (1,)), ((), ())), preferred_element_type=F32)


def tile_and_product(inverse_ref, cols_ref, rows_ref, tile_ref, rows, add):
    feats, width = inverse_ref.shape
    inverse = inverse_ref[...]
    nrows = rows_ref.shape[0]
    for index in range(nrows):
        rows[:, index * width:(index + 1) * width] = augmented(rows_ref[index, :feats, :], inverse, 3)
    vectors = jnp.concatenate([rows_ref[index, feats:, :] for index in range(nrows)], axis=1)
    for begin in range(0, cols_ref.shape[0], CHUNK):
        inner = jnp.dot(cols_ref[begin:begin + CHUNK, :], rows[...], preferred_element_type=F32)
        tile = jnp.exp(inner).astype(BF16)
        tile_ref[begin:begin + CHUNK, :] = tile
        part = dot_last(vectors, tile)
        for index in range(CHUNK // width):
            add(begin // width + index, part[:, index * width:(index + 1) * width])


def near_product(inverse_ref, cols_ref, rows_ref, tile_ref, sums_ref, rows):
    def add(index, piece):
        sums_ref[index] = piece

    tile_and_product(inverse_ref, cols_ref, rows_ref, tile_ref, rows, add)


def far_product(inverse_ref, cols_ref, rows_ref, sums_ref, tile_ref, out_ref, rows):
    ncols, probes, _ = sums_ref.shape

    def add(index, piece):
        value = sums_ref[index] + piece
        high = value.astype(BF16)
        for peer in range(ncols):
            out_ref[peer, index * probes:(index + 1) * probes, :] = high
        out_ref[index, ncols * probes:(ncols + 1) * probes, :] = high
        out_ref[index, (ncols + 1) * probes:, :] = (value - high.astype(F32)).astype(BF16)

    tile_and_product(inverse_ref, cols_ref, rows_ref, tile_ref, rows, add)


def spread(factor, parts_ref, image_ref, out_ref):
    probes = image_ref.shape[0]
    begin = parts_ref.shape[1] - 2 * probes
    own = jnp.zeros(image_ref.shape, F32)
    for peer in range(parts_ref.shape[0]):
        own += parts_ref[peer, begin:begin + probes, :].astype(F32) + parts_ref[peer, begin + probes:, :].astype(F32)
    image = own * factor
    image_ref[...] = image
    small = image.astype(BF16)
    for index in range(out_ref.shape[0]):
        out_ref[index] = small


def placed(values, shape):
    lane = lax.broadcasted_iota(jnp.int32, shape, 1)
    row = lax.broadcasted_iota(jnp.int32, shape, 0)
    grid = jnp.zeros(shape, F32)
    for index, value in values:
        grid = jnp.where(lane == row + index * shape[0], value, grid)
    return jnp.sum(grid, axis=0, keepdims=True)


def column_images(factor, parts_ref, right_ref, image_ref, cols_ref, local_ref):
    probes = right_ref.shape[0]
    for index in range(cols_ref.shape[0]):
        total = jnp.zeros(right_ref.shape, F32)
        for peer in range(parts_ref.shape[0]):
            total += parts_ref[peer, index * probes:(index + 1) * probes, :].astype(F32)
        cols_ref[index] = total * factor
    right, image = right_ref[...], image_ref[...]
    pairs = ((right, right), (right, image), (image, image))
    sums = [(k, jnp.sum(a * b, axis=1, keepdims=True)) for k, (a, b) in enumerate(pairs)]
    local_ref[...] = placed(sums, right.shape)


def second_product(tile_ref, rows_ref, sums_ref):
    width = rows_ref.shape[2]
    vectors = jnp.concatenate([rows_ref[index] for index in range(rows_ref.shape[0])], axis=1)
    part = dot_last(vectors, tile_ref[...])
    for index in range(sums_ref.shape[0]):
        sums_ref[index] = part[:, index * width:(index + 1) * width]


def third_product(factor, tile_ref, rows_ref, start_ref, images_ref, local_ref, out_ref):
    ncols, probes, width = start_ref.shape
    vectors = jnp.concatenate([rows_ref[index] for index in range(rows_ref.shape[0])], axis=1)
    part = dot_last(vectors, tile_ref[...])
    total = jnp.zeros((probes, width), F32)
    for index in range(ncols):
        second = (start_ref[index] + part[:, index * width:(index + 1) * width]) * factor
        out_ref[index, :probes, :] = second
        total += second * images_ref[index]
    energy = placed([(3, jnp.sum(total, axis=1, keepdims=True))], (probes, width))
    row = lax.broadcasted_iota(jnp.int32, (PAD, width), 0)
    scalars = jnp.where(row == 0, energy + local_ref[...], 0.0)
    for index in range(ncols):
        out_ref[index, probes:, :] = scalars


def gathered(parts_ref, second_ref, out_ref):
    total = jnp.sum(parts_ref[...], axis=0)
    probes = second_ref.shape[0]
    second_ref[...] = total[:probes]
    out_ref[...] = jnp.broadcast_to(total[probes:probes + 1], out_ref.shape)


def finish(all_ref, right_ref, image_ref, second_ref, solution_ref, residual_ref):
    right, image, second = right_ref[...], image_ref[...], second_ref[...]
    totals = jnp.sum(all_ref[...], axis=0, keepdims=True)
    lane = lax.broadcasted_iota(jnp.int32, right.shape, 1)
    row = lax.broadcasted_iota(jnp.int32, right.shape, 0)

    def moment(index):
        return jnp.sum(jnp.where(lane == row + index * right.shape[0], totals, 0.0), axis=1, keepdims=True)

    bb, bu, uu, uw = [moment(index) for index in range(4)]
    curve = bb + bu
    alpha = bb / curve
    rest = bu / curve
    norm = rest * rest * bb - 2.0 * alpha * rest * bu + alpha * alpha * uu
    lead = rest + norm / bb
    bend = (
        lead * lead * bb - 2.0 * lead * alpha * bu + alpha * alpha * uu
        + lead * (lead * bu - alpha * uu) - alpha * (lead * uu - alpha * uw)
    )
    later = norm / bend
    direction = lead * right - alpha * image
    solution_ref[...] = alpha * right + later * direction
    residual_ref[...] = right - alpha * (right + image) - later * (direction + lead * image - alpha * second)


def per_device(features, lengthscale, right_side):
    nx, nz, ncore, ny = [lax.axis_size(axis) for axis in AXES]
    feats, width = features.shape
    probes = right_side.shape[0]
    plane = nx * nz
    factor = float(width * plane * ncore * ny) ** (-0.5)
    block = shaped(F32, probes, width)
    swap = [(0, 1), (1, 0)]

    def exchange(values, axes):
        return lax.all_to_all(values, axes, 0, 0, tiled=True)

    def held(array):
        return pltpu.with_memory_space_constraint(array, pltpu.VMEM)

    cols, rows, right = call(
        copies, *[pltpu.with_memory_space_constraint(array, pltpu.HBM) for array in (features, right_side)], specs=[pl.BlockSpec(memory_space=pltpu.HBM)] * 2,
        outs=[shaped(BF16, ny, feats, width), pltpu.VMEM((plane, feats + probes, width), BF16), pltpu.VMEM(block.shape, F32)],
        scratch=[pltpu.VMEM(features.shape, BF16), pltpu.SemaphoreType.DMA((2,))],
    )
    right = held(right)
    cols = exchange(cols, "y")
    rows, cols = lax.optimization_barrier((rows, cols))
    near = exchange(rows, ("x", "z"))
    inverse, cols = call(
        columns, lengthscale.reshape(1, feats), cols,
        outs=[shaped(F32, feats, width), shaped(BF16, ny * width, feats + EXTRA)],
    )
    near, inverse, cols = lax.optimization_barrier((near, inverse, cols))
    far = lax.ppermute(near, "core", swap)
    tile = pltpu.VMEM((ny * width, plane * width), BF16)
    scratch = [pltpu.VMEM((feats + EXTRA, plane * width), BF16)]
    tile_near, sums = call(
        near_product, inverse, cols, near, outs=[tile, shaped(F32, ny, probes, width)], limit=24, scratch=scratch
    )
    tile_far, parts = call(
        far_product, inverse, cols, far, sums, outs=[tile, shaped(BF16, ny, (ny + 2) * probes, width)],
        limit=24, scratch=scratch,
    )
    parts = exchange(parts, "y")
    image, rows = call(
        functools.partial(spread, factor), parts, outs=[block, shaped(BF16, plane, probes, width)]
    )
    near = exchange(rows, ("x", "z"))
    images, local = call(
        functools.partial(column_images, factor), parts, right, image,
        outs=[shaped(F32, ny, probes, width), shaped(F32, 1, width)],
    )
    far = lax.ppermute(near, "core", swap)
    sums = call(second_product, held(tile_near), near, outs=shaped(F32, ny, probes, width))
    sums = call(
        functools.partial(third_product, factor), held(tile_far), far, sums, images, local,
        outs=shaped(F32, ny, probes + PAD, width),
    )
    second, local = call(gathered, exchange(sums, "y"), outs=[block, shaped(F32, plane * ncore, width)])
    everyone = exchange(local, ("x", "z", "core"))
    return call(finish, everyone, right, image, second, outs=[block, block])


def solution(mesh):
    fine = Mesh(mesh.devices.reshape(4, 8, 2, 8), AXES)
    split = P(None, AXES)
    return jax.shard_map(
        per_device,
        mesh=fine,
        in_specs=(split, P(), split),
        out_specs=(split, split),
        check_vma=False,
    )
```

```python
import functools

import jax
import jax.numpy as jnp
from jax import lax
from jax.experimental import pallas as pl
from jax.experimental.pallas import tpu as pltpu
from jax.sharding import Mesh, PartitionSpec as P

F32, BF16 = jnp.float32, jnp.bfloat16
EXTRA = 16
PAD = 8
CHUNK = 1024
AXES = ("x", "z", "core", "y")
VMEM = pl.BlockSpec(memory_space=pltpu.VMEM)


def call(kernel, *args, outs, limit=16, scratch=(), specs=None):
    return pl.pallas_call(
        kernel,
        in_specs=specs or [VMEM] * len(args),
        out_specs=jax.tree.map(lambda _: VMEM, outs),
        out_shape=outs,
        scratch_shapes=scratch,
        compiler_params=pltpu.CompilerParams(vmem_limit_bytes=limit << 20),
    )(*args)


def shaped(dtype, *shape):
    return jax.ShapeDtypeStruct(shape, dtype)


def pieces(value):
    high = value.astype(BF16).astype(F32)
    middle = (value - high).astype(BF16).astype(F32)
    return high, middle, value - high - middle


def augmented(raw, inverse, offset):
    scaled = (raw.astype(F32) * inverse).astype(BF16)
    wide = scaled.astype(F32)
    half = jnp.sum(wide * wide, axis=0, keepdims=True) * -0.5
    high, middle, low = pieces(half)
    row = lax.broadcasted_iota(jnp.int32, (EXTRA, raw.shape[1]), 0)
    below = jnp.where(row < 6, 1.0, 0.0)
    for index, part in enumerate((high, middle, low)):
        below = jnp.where(row == offset + index, part, below)
    return jnp.concatenate([scaled, below.astype(BF16)], axis=0)


def copies(features_ref, right_ref, cols_ref, rows_ref, kept_ref, held, sems):
    moves = [
        pltpu.make_async_copy(features_ref, held, sems.at[0]),
        pltpu.make_async_copy(right_ref, kept_ref, sems.at[1]),
    ]
    for move in moves:
        move.start()
    for move in moves:
        move.wait()
    features, right = held[...], kept_ref[...].astype(BF16)
    feats = features.shape[0]
    for index in range(cols_ref.shape[0]):
        cols_ref[index] = features
    for index in range(rows_ref.shape[0]):
        rows_ref[index, :feats, :] = features
        rows_ref[index, feats:, :] = right


def columns(scale_ref, cols_ref, inverse_ref, out_ref):
    ncols, feats, width = cols_ref.shape
    lane = lax.broadcasted_iota(jnp.int32, (feats, feats), 1)
    row = lax.broadcasted_iota(jnp.int32, (feats, feats), 0)
    scale = jnp.sum(jnp.where(lane == row, scale_ref[...], 0.0), axis=1, keepdims=True)
    inverse = jnp.broadcast_to(1.0 / scale, (feats, width))
    inverse_ref[...] = inverse
    for index in range(ncols):
        block = augmented(cols_ref[index], inverse, 0).astype(F32)
        out_ref[index * width:(index + 1) * width, :] = jnp.transpose(block).astype(BF16)


def dot_last(left, right):
    return lax.dot_general(left, right, (((1,), (1,)), ((), ())), preferred_element_type=F32)


def tile_and_product(inverse_ref, cols_ref, rows_ref, tile_ref, rows, add):
    feats, width = inverse_ref.shape
    inverse = inverse_ref[...]
    nrows = rows_ref.shape[0]
    for index in range(nrows):
        rows[:, index * width:(index + 1) * width] = augmented(rows_ref[index, :feats, :], inverse, 3)
    vectors = jnp.concatenate([rows_ref[index, feats:, :] for index in range(nrows)], axis=1)
    for begin in range(0, cols_ref.shape[0], CHUNK):
        inner = jnp.dot(cols_ref[begin:begin + CHUNK, :], rows[...], preferred_element_type=F32)
        tile = jnp.exp(inner).astype(BF16)
        tile_ref[begin:begin + CHUNK, :] = tile
        part = dot_last(vectors, tile)
        for index in range(CHUNK // width):
            add(begin // width + index, part[:, index * width:(index + 1) * width])


def near_product(inverse_ref, cols_ref, rows_ref, tile_ref, sums_ref, rows):
    def add(index, piece):
        sums_ref[index] = piece

    tile_and_product(inverse_ref, cols_ref, rows_ref, tile_ref, rows, add)


def far_product(inverse_ref, cols_ref, rows_ref, sums_ref, tile_ref, out_ref, rows):
    ncols, probes, _ = sums_ref.shape

    def add(index, piece):
        value = sums_ref[index] + piece
        high = value.astype(BF16)
        for peer in range(ncols):
            out_ref[peer, index * probes:(index + 1) * probes, :] = high
        out_ref[index, ncols * probes:(ncols + 1) * probes, :] = high
        out_ref[index, (ncols + 1) * probes:, :] = (value - high.astype(F32)).astype(BF16)

    tile_and_product(inverse_ref, cols_ref, rows_ref, tile_ref, rows, add)


def spread(factor, parts_ref, image_ref, out_ref):
    probes = image_ref.shape[0]
    begin = parts_ref.shape[1] - 2 * probes
    own = jnp.zeros(image_ref.shape, F32)
    for peer in range(parts_ref.shape[0]):
        own += parts_ref[peer, begin:begin + probes, :].astype(F32) + parts_ref[peer, begin + probes:, :].astype(F32)
    image = own * factor
    image_ref[...] = image
    small = image.astype(BF16)
    for index in range(out_ref.shape[0]):
        out_ref[index] = small


def placed(values, shape):
    lane = lax.broadcasted_iota(jnp.int32, shape, 1)
    row = lax.broadcasted_iota(jnp.int32, shape, 0)
    grid = jnp.zeros(shape, F32)
    for index, value in values:
        grid = jnp.where(lane == row + index * shape[0], value, grid)
    return jnp.sum(grid, axis=0, keepdims=True)


def column_images(factor, parts_ref, right_ref, image_ref, cols_ref, local_ref):
    probes = right_ref.shape[0]
    for index in range(cols_ref.shape[0]):
        total = jnp.zeros(right_ref.shape, F32)
        for peer in range(parts_ref.shape[0]):
            total += parts_ref[peer, index * probes:(index + 1) * probes, :].astype(F32)
        cols_ref[index] = total * factor
    right, image = right_ref[...], image_ref[...]
    pairs = ((right, right), (right, image), (image, image))
    sums = [(k, jnp.sum(a * b, axis=1, keepdims=True)) for k, (a, b) in enumerate(pairs)]
    local_ref[...] = placed(sums, right.shape)


def second_product(tile_ref, rows_ref, sums_ref):
    width = rows_ref.shape[2]
    vectors = jnp.concatenate([rows_ref[index] for index in range(rows_ref.shape[0])], axis=1)
    part = dot_last(vectors, tile_ref[...])
    for index in range(sums_ref.shape[0]):
        sums_ref[index] = part[:, index * width:(index + 1) * width]


def third_product(factor, tile_ref, rows_ref, start_ref, images_ref, local_ref, out_ref):
    ncols, probes, width = start_ref.shape
    vectors = jnp.concatenate([rows_ref[index] for index in range(rows_ref.shape[0])], axis=1)
    part = dot_last(vectors, tile_ref[...])
    total = jnp.zeros((probes, width), F32)
    for index in range(ncols):
        second = (start_ref[index] + part[:, index * width:(index + 1) * width]) * factor
        out_ref[index, :probes, :] = second
        total += second * images_ref[index]
    energy = placed([(3, jnp.sum(total, axis=1, keepdims=True))], (probes, width))
    row = lax.broadcasted_iota(jnp.int32, (PAD, width), 0)
    scalars = jnp.where(row == 0, energy + local_ref[...], 0.0)
    for index in range(ncols):
        out_ref[index, probes:, :] = scalars


def gathered(parts_ref, second_ref, out_ref):
    total = jnp.sum(parts_ref[...], axis=0)
    probes = second_ref.shape[0]
    second_ref[...] = total[:probes]
    out_ref[...] = jnp.broadcast_to(total[probes:probes + 1], out_ref.shape)


def finish(all_ref, right_ref, image_ref, second_ref, solution_ref, residual_ref):
    right, image, second = right_ref[...], image_ref[...], second_ref[...]
    totals = jnp.sum(all_ref[...], axis=0, keepdims=True)
    lane = lax.broadcasted_iota(jnp.int32, right.shape, 1)
    row = lax.broadcasted_iota(jnp.int32, right.shape, 0)

    def moment(index):
        return jnp.sum(jnp.where(lane == row + index * right.shape[0], totals, 0.0), axis=1, keepdims=True)

    bb, bu, uu, uw = [moment(index) for index in range(4)]
    curve = bb + bu
    alpha = bb / curve
    rest = bu / curve
    norm = rest * rest * bb - 2.0 * alpha * rest * bu + alpha * alpha * uu
    lead = rest + norm / bb
    bend = (
        lead * lead * bb - 2.0 * lead * alpha * bu + alpha * alpha * uu
        + lead * (lead * bu - alpha * uu) - alpha * (lead * uu - alpha * uw)
    )
    later = norm / bend
    direction = lead * right - alpha * image
    solution_ref[...] = alpha * right + later * direction
    residual_ref[...] = right - alpha * (right + image) - later * (direction + lead * image - alpha * second)


def per_device(features, lengthscale, right_side):
    nx, nz, ncore, ny = [lax.axis_size(axis) for axis in AXES]
    feats, width = features.shape
    probes = right_side.shape[0]
    plane = nx * nz
    factor = float(width * plane * ncore * ny) ** (-0.5)
    block = shaped(F32, probes, width)
    swap = [(0, 1), (1, 0)]

    def exchange(values, axes):
        return lax.all_to_all(values, axes, 0, 0, tiled=True)

    def held(array):
        return pltpu.with_memory_space_constraint(array, pltpu.VMEM)

    cols, rows, right = call(
        copies, *[pltpu.with_memory_space_constraint(array, pltpu.HBM) for array in (features, right_side)], specs=[pl.BlockSpec(memory_space=pltpu.HBM)] * 2,
        outs=[shaped(BF16, ny, feats, width), pltpu.VMEM((plane, feats + probes, width), BF16), pltpu.VMEM(block.shape, F32)],
        scratch=[pltpu.VMEM(features.shape, BF16), pltpu.SemaphoreType.DMA((2,))],
    )
    right = held(right)
    cols = exchange(cols, "y")
    rows, cols = lax.optimization_barrier((rows, cols))
    near = exchange(rows, ("x", "z"))
    inverse, cols = call(
        columns, lengthscale.reshape(1, feats), cols,
        outs=[shaped(F32, feats, width), shaped(BF16, ny * width, feats + EXTRA)],
    )
    near, inverse, cols = lax.optimization_barrier((near, inverse, cols))
    far = lax.ppermute(near, "core", swap)
    tile = pltpu.VMEM((ny * width, plane * width), BF16)
    scratch = [pltpu.VMEM((feats + EXTRA, plane * width), BF16)]
    tile_near, sums = call(
        near_product, inverse, cols, near, outs=[tile, shaped(F32, ny, probes, width)], limit=24, scratch=scratch
    )
    tile_far, parts = call(
        far_product, inverse, cols, far, sums, outs=[tile, shaped(BF16, ny, (ny + 2) * probes, width)],
        limit=24, scratch=scratch,
    )
    parts = exchange(parts, "y")
    image, rows = call(
        functools.partial(spread, factor), parts, outs=[block, shaped(BF16, plane, probes, width)]
    )
    near = exchange(rows, ("x", "z"))
    images, local = call(
        functools.partial(column_images, factor), parts, right, image,
        outs=[shaped(F32, ny, probes, width), shaped(F32, 1, width)],
    )
    far = lax.ppermute(near, "core", swap)
    sums = call(second_product, held(tile_near), near, outs=shaped(F32, ny, probes, width))
    sums = call(
        functools.partial(third_product, factor), held(tile_far), far, sums, images, local,
        outs=shaped(F32, ny, probes + PAD, width),
    )
    second, local = call(gathered, exchange(sums, "y"), outs=[block, shaped(F32, plane * ncore, width)])
    everyone = exchange(local, ("x", "z", "core"))
    return call(finish, everyone, right, image, second, outs=[block, block])


def solution(mesh):
    fine = Mesh(mesh.devices.reshape(4, 8, 2, 8), AXES)
    split = P(None, AXES)
    return jax.shard_map(
        per_device,
        mesh=fine,
        in_specs=(split, P(), split),
        out_specs=(split, split),
        check_vma=False,
    )
```

```python
import functools

import jax
import jax.numpy as jnp
from jax import lax
from jax.experimental import pallas as pl
from jax.experimental.pallas import tpu as pltpu
from jax.sharding import Mesh, PartitionSpec as P

F32, BF16 = jnp.float32, jnp.bfloat16
EXTRA = 16
PAD = 8
CHUNK = 1024
AXES = ("x", "z", "core", "y")
VMEM = pl.BlockSpec(memory_space=pltpu.VMEM)


def call(kernel, *args, outs, limit=16, scratch=(), specs=None):
    return pl.pallas_call(
        kernel,
        in_specs=specs or [VMEM] * len(args),
        out_specs=jax.tree.map(lambda _: VMEM, outs),
        out_shape=outs,
        scratch_shapes=scratch,
        compiler_params=pltpu.CompilerParams(vmem_limit_bytes=limit << 20),
    )(*args)


def shaped(dtype, *shape):
    return jax.ShapeDtypeStruct(shape, dtype)


def pieces(value):
    high = value.astype(BF16).astype(F32)
    middle = (value - high).astype(BF16).astype(F32)
    return high, middle, value - high - middle


def augmented(raw, inverse, offset):
    scaled = (raw.astype(F32) * inverse).astype(BF16)
    wide = scaled.astype(F32)
    half = jnp.sum(wide * wide, axis=0, keepdims=True) * -0.5
    high, middle, low = pieces(half)
    row = lax.broadcasted_iota(jnp.int32, (EXTRA, raw.shape[1]), 0)
    below = jnp.where(row < 6, 1.0, 0.0)
    for index, part in enumerate((high, middle, low)):
        below = jnp.where(row == offset + index, part, below)
    return jnp.concatenate([scaled, below.astype(BF16)], axis=0)


def column_copies(features_ref, cols_ref, held, sem):
    move = pltpu.make_async_copy(features_ref, held, sem)
    move.start()
    move.wait()
    features = held[...]
    for index in range(cols_ref.shape[0]):
        cols_ref[index] = features


def row_copies(features_ref, right_ref, rows_ref, kept_ref, held, sems):
    moves = [
        pltpu.make_async_copy(features_ref, held, sems.at[0]),
        pltpu.make_async_copy(right_ref, kept_ref, sems.at[1]),
    ]
    for move in moves:
        move.start()
    for move in moves:
        move.wait()
    features, right = held[...], kept_ref[...].astype(BF16)
    feats = features.shape[0]
    for index in range(rows_ref.shape[0]):
        rows_ref[index, :feats, :] = features
        rows_ref[index, feats:, :] = right


def columns(scale_ref, cols_ref, inverse_ref, out_ref):
    ncols, feats, width = cols_ref.shape
    lane = lax.broadcasted_iota(jnp.int32, (feats, feats), 1)
    row = lax.broadcasted_iota(jnp.int32, (feats, feats), 0)
    scale = jnp.sum(jnp.where(lane == row, scale_ref[...], 0.0), axis=1, keepdims=True)
    inverse = jnp.broadcast_to(1.0 / scale, (feats, width))
    inverse_ref[...] = inverse
    for index in range(ncols):
        block = augmented(cols_ref[index], inverse, 0).astype(F32)
        out_ref[index * width:(index + 1) * width, :] = jnp.transpose(block).astype(BF16)


def dot_last(left, right):
    return lax.dot_general(left, right, (((1,), (1,)), ((), ())), preferred_element_type=F32)


def tile_and_product(inverse_ref, cols_ref, rows_ref, tile_ref, rows, add):
    feats, width = inverse_ref.shape
    inverse = inverse_ref[...]
    nrows = rows_ref.shape[0]
    for index in range(nrows):
        rows[:, index * width:(index + 1) * width] = augmented(rows_ref[index, :feats, :], inverse, 3)
    vectors = jnp.concatenate([rows_ref[index, feats:, :] for index in range(nrows)], axis=1)
    for begin in range(0, cols_ref.shape[0], CHUNK):
        inner = jnp.dot(cols_ref[begin:begin + CHUNK, :], rows[...], preferred_element_type=F32)
        tile = jnp.exp(inner).astype(BF16)
        tile_ref[begin:begin + CHUNK, :] = tile
        part = dot_last(vectors, tile)
        for index in range(CHUNK // width):
            add(begin // width + index, part[:, index * width:(index + 1) * width])


def near_product(inverse_ref, cols_ref, rows_ref, tile_ref, sums_ref, rows):
    def add(index, piece):
        sums_ref[index] = piece

    tile_and_product(inverse_ref, cols_ref, rows_ref, tile_ref, rows, add)


def far_product(inverse_ref, cols_ref, rows_ref, sums_ref, tile_ref, out_ref, rows):
    ncols, probes, _ = sums_ref.shape

    def add(index, piece):
        value = sums_ref[index] + piece
        high = value.astype(BF16)
        for peer in range(ncols):
            out_ref[peer, index * probes:(index + 1) * probes, :] = high
        out_ref[index, ncols * probes:, :] = (value - high.astype(F32)).astype(BF16)

    tile_and_product(inverse_ref, cols_ref, rows_ref, tile_ref, rows, add)


def spread(factor, parts_ref, image_ref, out_ref):
    probes = image_ref.shape[0]
    last = parts_ref.shape[1] - probes
    mine = pl.ds(pl.multiple_of(lax.axis_index("y") * probes, probes), probes)
    own = jnp.zeros(image_ref.shape, F32)
    for peer in range(parts_ref.shape[0]):
        own += parts_ref[peer, mine, :].astype(F32) + parts_ref[peer, last:, :].astype(F32)
    image = own * factor
    image_ref[...] = image
    small = image.astype(BF16)
    for index in range(out_ref.shape[0]):
        out_ref[index] = small


def placed(values, shape):
    lane = lax.broadcasted_iota(jnp.int32, shape, 1)
    row = lax.broadcasted_iota(jnp.int32, shape, 0)
    grid = jnp.zeros(shape, F32)
    for index, value in values:
        grid = jnp.where(lane == row + index * shape[0], value, grid)
    return jnp.sum(grid, axis=0, keepdims=True)


def second_product(factor, near_ref, far_ref, rows_ref, parts_ref, right_ref, image_ref, out_ref):
    ncols = out_ref.shape[0]
    probes, width = right_ref.shape
    me = lax.axis_index("core")
    part = jnp.zeros((probes, ncols * width), F32)
    for half, tile_ref in ((me, near_ref), (1 - me, far_ref)):
        vectors = jnp.concatenate([rows_ref[half, index] for index in range(rows_ref.shape[1])], axis=1)
        part += dot_last(vectors, tile_ref[...])
    total = jnp.zeros((probes, width), F32)
    for index in range(ncols):
        first = jnp.zeros((probes, width), F32)
        for peer in range(parts_ref.shape[0]):
            first += parts_ref[peer, index * probes:(index + 1) * probes, :].astype(F32)
        second = part[:, index * width:(index + 1) * width] * factor
        out_ref[index, :probes, :] = second
        total += first * second
    right, image = right_ref[...], image_ref[...]
    products = (right * right, right * image, image * image, total * factor)
    sums = [(index, jnp.sum(product, axis=1, keepdims=True)) for index, product in enumerate(products)]
    row = lax.broadcasted_iota(jnp.int32, (PAD, width), 0)
    scalars = jnp.where(row == 0, placed(sums, (probes, width)), 0.0)
    for index in range(ncols):
        out_ref[index, probes:, :] = scalars


def gathered(parts_ref, second_ref, out_ref):
    total = jnp.sum(parts_ref[...], axis=0)
    probes = second_ref.shape[0]
    second_ref[...] = total[:probes]
    out_ref[...] = jnp.broadcast_to(total[probes:probes + 1], out_ref.shape)


def finish(all_ref, right_ref, image_ref, second_ref, solution_ref, residual_ref):
    right, image, second = right_ref[...], image_ref[...], second_ref[...]
    totals = jnp.sum(all_ref[...], axis=0, keepdims=True)
    lane = lax.broadcasted_iota(jnp.int32, right.shape, 1)
    row = lax.broadcasted_iota(jnp.int32, right.shape, 0)

    def moment(index):
        return jnp.sum(jnp.where(lane == row + index * right.shape[0], totals, 0.0), axis=1, keepdims=True)

    bb, bu, uu, uw = [moment(index) for index in range(4)]
    curve = bb + bu
    alpha = bb / curve
    rest = bu / curve
    norm = rest * rest * bb - 2.0 * alpha * rest * bu + alpha * alpha * uu
    lead = rest + norm / bb
    bend = (
        lead * lead * bb - 2.0 * lead * alpha * bu + alpha * alpha * uu
        + lead * (lead * bu - alpha * uu) - alpha * (lead * uu - alpha * uw)
    )
    later = norm / bend
    direction = lead * right - alpha * image
    solution_ref[...] = alpha * right + later * direction
    residual_ref[...] = right - alpha * (right + image) - later * (direction + lead * image - alpha * second)


def per_device(features, lengthscale, right_side):
    nx, nz, ncore, ny = [lax.axis_size(axis) for axis in AXES]
    feats, width = features.shape
    probes = right_side.shape[0]
    plane = nx * nz
    factor = float(width * plane * ncore * ny) ** (-0.5)
    block = shaped(F32, probes, width)
    swap = [(0, 1), (1, 0)]

    def exchange(values, axes):
        return lax.all_to_all(values, axes, 0, 0, tiled=True)

    def held(array):
        return pltpu.with_memory_space_constraint(array, pltpu.VMEM)

    source, given = [pltpu.with_memory_space_constraint(array, pltpu.HBM) for array in (features, right_side)]
    far_off = pl.BlockSpec(memory_space=pltpu.HBM)
    cols = call(
        column_copies, source, specs=[far_off], outs=shaped(BF16, ny, feats, width),
        scratch=[pltpu.VMEM(features.shape, BF16), pltpu.SemaphoreType.DMA],
    )
    cols = exchange(cols, "y")
    rows, right = call(
        row_copies, source, given, specs=[far_off] * 2,
        outs=[shaped(BF16, plane, feats + probes, width), pltpu.VMEM(block.shape, F32)],
        scratch=[pltpu.VMEM(features.shape, BF16), pltpu.SemaphoreType.DMA((2,))],
    )
    right = held(right)
    rows, cols = lax.optimization_barrier((rows, cols))
    near = exchange(rows, ("x", "z"))
    inverse, cols = call(
        columns, lengthscale.reshape(1, feats), cols,
        outs=[shaped(F32, feats, width), shaped(BF16, ny * width, feats + EXTRA)],
    )
    near, inverse, cols = lax.optimization_barrier((near, inverse, cols))
    far = lax.ppermute(near, "core", swap)
    tile = pltpu.VMEM((ny * width, plane * width), BF16)
    scratch = [pltpu.VMEM((feats + EXTRA, plane * width), BF16)]
    tile_near, sums = call(
        near_product, inverse, cols, near, outs=[tile, shaped(F32, ny, probes, width)], limit=24, scratch=scratch
    )
    tile_far, parts = call(
        far_product, inverse, cols, far, sums, outs=[tile, shaped(BF16, ny, (ny + 1) * probes, width)],
        limit=24, scratch=scratch,
    )
    parts = exchange(parts, "y")
    image, rows = call(
        functools.partial(spread, factor), parts, outs=[block, shaped(BF16, plane, probes, width)]
    )
    both = lax.all_gather(exchange(rows, ("x", "z")), "core")
    sums = call(
        functools.partial(second_product, factor), held(tile_near), held(tile_far), both, parts, right, image,
        outs=shaped(F32, ny, probes + PAD, width),
    )
    second, local = call(gathered, exchange(sums, "y"), outs=[block, shaped(F32, plane * ncore, width)])
    everyone = exchange(local, ("x", "z", "core"))
    return call(finish, everyone, right, image, second, outs=[block, block])


def solution(mesh):
    fine = Mesh(mesh.devices.reshape(4, 8, 2, 8), AXES)
    split = P(None, AXES)
    return jax.shard_map(
        per_device,
        mesh=fine,
        in_specs=(split, P(), split),
        out_specs=(split, split),
        check_vma=False,
    )
```

```python
import functools

import jax
import jax.numpy as jnp
from jax import lax
from jax.experimental import pallas as pl
from jax.experimental.pallas import tpu as pltpu
from jax.sharding import Mesh, PartitionSpec as P

F32, BF16 = jnp.float32, jnp.bfloat16
EXTRA = 16
PAD = 8
CHUNK = 1024
COLS = ("ya", "yb", "yc")
AXES = ("x", "z", "core") + COLS
VMEM = pl.BlockSpec(memory_space=pltpu.VMEM)


def call(kernel, *args, outs, limit=16, scratch=(), specs=None):
    return pl.pallas_call(
        kernel,
        in_specs=specs or [VMEM] * len(args),
        out_specs=jax.tree.map(lambda _: VMEM, outs),
        out_shape=outs,
        scratch_shapes=scratch,
        compiler_params=pltpu.CompilerParams(vmem_limit_bytes=limit << 20),
    )(*args)


def shaped(dtype, *shape):
    return jax.ShapeDtypeStruct(shape, dtype)


def pieces(value):
    high = value.astype(BF16).astype(F32)
    middle = (value - high).astype(BF16).astype(F32)
    return high, middle, value - high - middle


def augmented(raw, inverse, offset):
    scaled = (raw.astype(F32) * inverse).astype(BF16)
    wide = scaled.astype(F32)
    half = jnp.sum(wide * wide, axis=0, keepdims=True) * -0.5
    high, middle, low = pieces(half)
    row = lax.broadcasted_iota(jnp.int32, (EXTRA, raw.shape[1]), 0)
    below = jnp.where(row < 6, 1.0, 0.0)
    for index, part in enumerate((high, middle, low)):
        below = jnp.where(row == offset + index, part, below)
    return jnp.concatenate([scaled, below.astype(BF16)], axis=0)


def row_copies(features_ref, right_ref, rows_ref, kept_ref, held, sems):
    moves = [
        pltpu.make_async_copy(features_ref, held, sems.at[0]),
        pltpu.make_async_copy(right_ref, kept_ref, sems.at[1]),
    ]
    for move in moves:
        move.start()
    for move in moves:
        move.wait()
    features, right = held[...], kept_ref[...].astype(BF16)
    feats = features.shape[0]
    for index in range(rows_ref.shape[0]):
        rows_ref[index, :feats, :] = features
        rows_ref[index, feats:, :] = right


def columns(order, scale_ref, cols_ref, inverse_ref, out_ref):
    ncols, feats, width = cols_ref.shape
    lane = lax.broadcasted_iota(jnp.int32, (feats, feats), 1)
    row = lax.broadcasted_iota(jnp.int32, (feats, feats), 0)
    scale = jnp.sum(jnp.where(lane == row, scale_ref[...], 0.0), axis=1, keepdims=True)
    inverse = jnp.broadcast_to(1.0 / scale, (feats, width))
    inverse_ref[...] = inverse
    for place, index in enumerate(order):
        block = augmented(cols_ref[place], inverse, 0).astype(F32)
        out_ref[index * width:(index + 1) * width, :] = jnp.transpose(block).astype(BF16)


def dot_last(left, right):
    return lax.dot_general(left, right, (((1,), (1,)), ((), ())), preferred_element_type=F32)


def tile_and_product(inverse_ref, cols_ref, rows_ref, tile_ref, rows, add):
    feats, width = inverse_ref.shape
    inverse = inverse_ref[...]
    nrows = rows_ref.shape[0]
    for index in range(nrows):
        rows[:, index * width:(index + 1) * width] = augmented(rows_ref[index, :feats, :], inverse, 3)
    vectors = jnp.concatenate([rows_ref[index, feats:, :] for index in range(nrows)], axis=1)
    for begin in range(0, cols_ref.shape[0], CHUNK):
        inner = jnp.dot(cols_ref[begin:begin + CHUNK, :], rows[...], preferred_element_type=F32)
        tile = jnp.exp(inner).astype(BF16)
        tile_ref[begin:begin + CHUNK, :] = tile
        part = dot_last(vectors, tile)
        for index in range(CHUNK // width):
            add(begin // width + index, part[:, index * width:(index + 1) * width])


def near_product(inverse_ref, cols_ref, rows_ref, tile_ref, sums_ref, rows):
    def add(index, piece):
        sums_ref[index] = piece

    tile_and_product(inverse_ref, cols_ref, rows_ref, tile_ref, rows, add)


def far_product(inverse_ref, cols_ref, rows_ref, sums_ref, tile_ref, out_ref, rows):
    ncols, probes, _ = sums_ref.shape

    def add(index, piece):
        value = sums_ref[index] + piece
        high = value.astype(BF16)
        for peer in range(ncols):
            out_ref[peer, index * probes:(index + 1) * probes, :] = high
        out_ref[index, ncols * probes:, :] = (value - high.astype(F32)).astype(BF16)

    tile_and_product(inverse_ref, cols_ref, rows_ref, tile_ref, rows, add)


def spread(factor, parts_ref, image_ref, out_ref):
    probes = image_ref.shape[0]
    last = parts_ref.shape[1] - probes
    mine = pl.ds(pl.multiple_of(lax.axis_index(COLS) * probes, probes), probes)
    own = jnp.zeros(image_ref.shape, F32)
    for peer in range(parts_ref.shape[0]):
        own += parts_ref[peer, mine, :].astype(F32) + parts_ref[peer, last:, :].astype(F32)
    image = own * factor
    image_ref[...] = image
    small = image.astype(BF16)
    for index in range(out_ref.shape[0]):
        out_ref[index] = small


def placed(values, shape):
    lane = lax.broadcasted_iota(jnp.int32, shape, 1)
    row = lax.broadcasted_iota(jnp.int32, shape, 0)
    grid = jnp.zeros(shape, F32)
    for index, value in values:
        grid = jnp.where(lane == row + index * shape[0], value, grid)
    return jnp.sum(grid, axis=0, keepdims=True)


def second_product(factor, near_ref, far_ref, rows_ref, parts_ref, right_ref, image_ref, out_ref):
    ncols = out_ref.shape[0]
    probes, width = right_ref.shape
    me = lax.axis_index("core")
    part = jnp.zeros((probes, ncols * width), F32)
    for half, tile_ref in ((me, near_ref), (1 - me, far_ref)):
        vectors = jnp.concatenate([rows_ref[half, index] for index in range(rows_ref.shape[1])], axis=1)
        part += dot_last(vectors, tile_ref[...])
    total = jnp.zeros((probes, width), F32)
    for index in range(ncols):
        first = jnp.zeros((probes, width), F32)
        for peer in range(parts_ref.shape[0]):
            first += parts_ref[peer, index * probes:(index + 1) * probes, :].astype(F32)
        second = part[:, index * width:(index + 1) * width] * factor
        out_ref[index, :probes, :] = second
        total += first * second
    right, image = right_ref[...], image_ref[...]
    products = (right * right, right * image, image * image, total * factor)
    sums = [(index, jnp.sum(product, axis=1, keepdims=True)) for index, product in enumerate(products)]
    row = lax.broadcasted_iota(jnp.int32, (PAD, width), 0)
    scalars = jnp.where(row == 0, placed(sums, (probes, width)), 0.0)
    for index in range(ncols):
        out_ref[index, probes:, :] = scalars


def gathered(parts_ref, second_ref, out_ref):
    total = jnp.sum(parts_ref[...], axis=0)
    probes = second_ref.shape[0]
    second_ref[...] = total[:probes]
    out_ref[...] = jnp.broadcast_to(total[probes:probes + 1], out_ref.shape)


def finish(all_ref, right_ref, image_ref, second_ref, solution_ref, residual_ref):
    right, image, second = right_ref[...], image_ref[...], second_ref[...]
    totals = jnp.sum(all_ref[...], axis=0, keepdims=True)
    lane = lax.broadcasted_iota(jnp.int32, right.shape, 1)
    row = lax.broadcasted_iota(jnp.int32, right.shape, 0)

    def moment(index):
        return jnp.sum(jnp.where(lane == row + index * right.shape[0], totals, 0.0), axis=1, keepdims=True)

    bb, bu, uu, uw = [moment(index) for index in range(4)]
    curve = bb + bu
    alpha = bb / curve
    rest = bu / curve
    norm = rest * rest * bb - 2.0 * alpha * rest * bu + alpha * alpha * uu
    lead = rest + norm / bb
    bend = (
        lead * lead * bb - 2.0 * lead * alpha * bu + alpha * alpha * uu
        + lead * (lead * bu - alpha * uu) - alpha * (lead * uu - alpha * uw)
    )
    later = norm / bend
    direction = lead * right - alpha * image
    solution_ref[...] = alpha * right + later * direction
    residual_ref[...] = right - alpha * (right + image) - later * (direction + lead * image - alpha * second)


def per_device(features, lengthscale, right_side):
    nx, nz, ncore = [lax.axis_size(axis) for axis in AXES[:3]]
    ny = lax.axis_size(COLS)
    feats, width = features.shape
    probes = right_side.shape[0]
    plane = nx * nz
    factor = float(width * plane * ncore * ny) ** (-0.5)
    block = shaped(F32, probes, width)
    swap = [(0, 1), (1, 0)]

    def exchange(values, axes):
        return lax.all_to_all(values, axes, 0, 0, tiled=True)

    def held(array):
        return pltpu.with_memory_space_constraint(array, pltpu.VMEM)

    source, given = [pltpu.with_memory_space_constraint(array, pltpu.HBM) for array in (features, right_side)]
    far_off = pl.BlockSpec(memory_space=pltpu.HBM)
    rows, right = call(
        row_copies, source, given, specs=[far_off] * 2,
        outs=[shaped(BF16, plane, feats + probes, width), pltpu.VMEM(block.shape, F32)],
        scratch=[pltpu.VMEM(features.shape, BF16), pltpu.SemaphoreType.DMA((2,))],
    )
    right = held(right)
    near = exchange(rows, ("x", "z"))
    cols = features[None]
    for axis in COLS:
        cols = lax.all_gather(cols, axis, axis=0, tiled=True)
    order = [sum(((place >> bit) & 1) << (len(COLS) - 1 - bit) for bit in range(len(COLS))) for place in range(ny)]
    inverse, cols = call(
        functools.partial(columns, order), lengthscale.reshape(1, feats), cols,
        outs=[shaped(F32, feats, width), shaped(BF16, ny * width, feats + EXTRA)],
    )
    near, inverse, cols = lax.optimization_barrier((near, inverse, cols))
    far = lax.ppermute(near, "core", swap)
    tile = pltpu.VMEM((ny * width, plane * width), BF16)
    scratch = [pltpu.VMEM((feats + EXTRA, plane * width), BF16)]
    tile_near, sums = call(
        near_product, inverse, cols, near, outs=[tile, shaped(F32, ny, probes, width)], limit=24, scratch=scratch
    )
    tile_far, parts = call(
        far_product, inverse, cols, far, sums, outs=[tile, shaped(BF16, ny, (ny + 1) * probes, width)],
        limit=24, scratch=scratch,
    )
    parts = exchange(parts, COLS)
    image, rows = call(
        functools.partial(spread, factor), parts, outs=[block, shaped(BF16, plane, probes, width)]
    )
    both = lax.all_gather(exchange(rows, ("x", "z")), "core")
    sums = call(
        functools.partial(second_product, factor), held(tile_near), held(tile_far), both, parts, right, image,
        outs=shaped(F32, ny, probes + PAD, width),
    )
    second, local = call(gathered, exchange(sums, COLS), outs=[block, shaped(F32, plane * ncore, width)])
    everyone = exchange(local, ("x", "z", "core"))
    return call(finish, everyone, right, image, second, outs=[block, block])


def solution(mesh):
    fine = Mesh(mesh.devices.reshape(4, 8, 2, 2, 2, 2), AXES)
    split = P(None, AXES)
    return jax.shard_map(
        per_device,
        mesh=fine,
        in_specs=(split, P(), split),
        out_specs=(split, split),
        check_vma=False,
    )
```

```python
import functools

import jax
import jax.numpy as jnp
from jax import lax
from jax.experimental import pallas as pl
from jax.experimental.pallas import tpu as pltpu
from jax.sharding import Mesh, PartitionSpec as P

F32, BF16 = jnp.float32, jnp.bfloat16
EXTRA = 16
PAD = 8
COLS = ("ya", "yb", "yc")
AXES = ("x", "z", "core") + COLS
VMEM = pl.BlockSpec(memory_space=pltpu.VMEM)


def call(kernel, *args, outs, limit=16, scratch=(), specs=None):
    return pl.pallas_call(
        kernel,
        in_specs=specs or [VMEM] * len(args),
        out_specs=jax.tree.map(lambda _: VMEM, outs),
        out_shape=outs,
        scratch_shapes=scratch,
        compiler_params=pltpu.CompilerParams(vmem_limit_bytes=limit << 20),
    )(*args)


def shaped(dtype, *shape):
    return jax.ShapeDtypeStruct(shape, dtype)


def pieces(value):
    high = value.astype(BF16).astype(F32)
    middle = (value - high).astype(BF16).astype(F32)
    return high, middle, value - high - middle


def augmented(raw, inverse, offset):
    scaled = (raw.astype(F32) * inverse).astype(BF16)
    wide = scaled.astype(F32)
    half = jnp.sum(wide * wide, axis=0, keepdims=True) * -0.5
    high, middle, low = pieces(half)
    row = lax.broadcasted_iota(jnp.int32, (EXTRA, raw.shape[1]), 0)
    below = jnp.where(row < 6, 1.0, 0.0)
    for index, part in enumerate((high, middle, low)):
        below = jnp.where(row == offset + index, part, below)
    return jnp.concatenate([scaled, below.astype(BF16)], axis=0)


def row_copies(features_ref, right_ref, rows_ref, kept_ref, held, sems):
    moves = [
        pltpu.make_async_copy(features_ref, held, sems.at[0]),
        pltpu.make_async_copy(right_ref, kept_ref, sems.at[1]),
    ]
    for move in moves:
        move.start()
    for move in moves:
        move.wait()
    features, right = held[...], kept_ref[...].astype(BF16)
    feats = features.shape[0]
    for index in range(rows_ref.shape[0]):
        rows_ref[index, :feats, :] = features
        rows_ref[index, feats:, :] = right


def put_columns(cols_ref, inverse, out_ref):
    ncols, _, width = cols_ref.shape
    for index in range(ncols):
        block = augmented(cols_ref[index % 2 * 2 + index // 2], inverse, 0).astype(F32)
        out_ref[index * width:(index + 1) * width, :] = jnp.transpose(block).astype(BF16)


def columns(scale_ref, cols_ref, inverse_ref, out_ref):
    _, feats, width = cols_ref.shape
    lane = lax.broadcasted_iota(jnp.int32, (feats, feats), 1)
    row = lax.broadcasted_iota(jnp.int32, (feats, feats), 0)
    scale = jnp.sum(jnp.where(lane == row, scale_ref[...], 0.0), axis=1, keepdims=True)
    inverse = jnp.broadcast_to(1.0 / scale, (feats, width))
    inverse_ref[...] = inverse
    put_columns(cols_ref, inverse, out_ref)


def dot_last(left, right):
    return lax.dot_general(left, right, (((1,), (1,)), ((), ())), preferred_element_type=F32)


def put_rows(rows_ref, inverse, out_ref):
    feats, width = inverse.shape
    for index in range(rows_ref.shape[0]):
        out_ref[:, index * width:(index + 1) * width] = augmented(rows_ref[index, :feats, :], inverse, 3)


def vectors_of(rows_ref, feats):
    return jnp.concatenate([rows_ref[index, feats:, :] for index in range(rows_ref.shape[0])], axis=1)


def tile_and_product(cols_ref, rows_ref, vectors, tile_ref):
    inner = jnp.dot(cols_ref[...], rows_ref[...], preferred_element_type=F32)
    tile = jnp.exp(inner).astype(BF16)
    tile_ref[...] = tile
    return dot_last(vectors, tile)


def own_near(inverse_ref, cols_ref, near_ref, tile_ref, sums_ref, rows_ref):
    put_rows(near_ref, inverse_ref[...], rows_ref)
    sums_ref[...] = tile_and_product(cols_ref, rows_ref, vectors_of(near_ref, inverse_ref.shape[0]), tile_ref)


def other_near(inverse_ref, raw_ref, near_ref, rows_ref, tile_ref, sums_ref, cols_ref):
    put_columns(raw_ref, inverse_ref[...], cols_ref)
    sums_ref[...] = tile_and_product(cols_ref, rows_ref, vectors_of(near_ref, inverse_ref.shape[0]), tile_ref)


def placing(ncols):
    me = lax.axis_index(COLS[2])
    half = ncols // 2
    return [index % half * 2 + (me if index < half else 1 - me) for index in range(ncols)]


def far_product(inverse_ref, own_ref, other_ref, far_ref, own_sums_ref, other_sums_ref, tile_ref, out_ref, rows, cols):
    probes = own_sums_ref.shape[0]
    ncols = out_ref.shape[0]
    feats, width = inverse_ref.shape
    middle = own_ref.shape[0]
    cols[:middle, :] = own_ref[...]
    cols[middle:, :] = other_ref[...]
    put_rows(far_ref, inverse_ref[...], rows)
    part = tile_and_product(cols, rows, vectors_of(far_ref, feats), tile_ref)
    part += jnp.concatenate([own_sums_ref[...], other_sums_ref[...]], axis=1)
    for index, place in enumerate(placing(ncols)):
        value = part[:, index * width:(index + 1) * width]
        high = value.astype(BF16)
        where = pl.ds(pl.multiple_of(place * probes, probes), probes)
        for peer in range(ncols):
            out_ref[peer, where, :] = high
        out_ref[place, ncols * probes:, :] = (value - high.astype(F32)).astype(BF16)


def spread(factor, parts_ref, image_ref, out_ref):
    probes = image_ref.shape[0]
    last = parts_ref.shape[1] - probes
    mine = pl.ds(pl.multiple_of(lax.axis_index(COLS) * probes, probes), probes)
    own = jnp.zeros(image_ref.shape, F32)
    for peer in range(parts_ref.shape[0]):
        own += parts_ref[peer, mine, :].astype(F32) + parts_ref[peer, last:, :].astype(F32)
    image = own * factor
    image_ref[...] = image
    small = image.astype(BF16)
    for index in range(out_ref.shape[0]):
        out_ref[index] = small


def placed(values, shape):
    lane = lax.broadcasted_iota(jnp.int32, shape, 1)
    row = lax.broadcasted_iota(jnp.int32, shape, 0)
    grid = jnp.zeros(shape, F32)
    for index, value in values:
        grid = jnp.where(lane == row + index * shape[0], value, grid)
    return jnp.sum(grid, axis=0, keepdims=True)


def second_product(factor, own_ref, other_ref, far_ref, rows_ref, parts_ref, right_ref, image_ref, out_ref):
    ncols = out_ref.shape[0]
    probes, width = right_ref.shape
    me = lax.axis_index("core")
    near, far = [
        jnp.concatenate([rows_ref[half, index] for index in range(rows_ref.shape[1])], axis=1) for half in (me, 1 - me)
    ]
    part = dot_last(far, far_ref[...])
    part += jnp.concatenate([dot_last(near, own_ref[...]), dot_last(near, other_ref[...])], axis=1)
    total = jnp.zeros((probes, width), F32)
    for index, place in enumerate(placing(ncols)):
        where = pl.ds(pl.multiple_of(place * probes, probes), probes)
        first = jnp.zeros((probes, width), F32)
        for peer in range(parts_ref.shape[0]):
            first += parts_ref[peer, where, :].astype(F32)
        second = part[:, index * width:(index + 1) * width] * factor
        out_ref[place, :probes, :] = second
        total += first * second
    right, image = right_ref[...], image_ref[...]
    products = (right * right, right * image, image * image, total * factor)
    sums = [(index, jnp.sum(product, axis=1, keepdims=True)) for index, product in enumerate(products)]
    row = lax.broadcasted_iota(jnp.int32, (PAD, width), 0)
    scalars = jnp.where(row == 0, placed(sums, (probes, width)), 0.0)
    for index in range(ncols):
        out_ref[index, probes:, :] = scalars


def gathered(parts_ref, second_ref, out_ref):
    total = jnp.sum(parts_ref[...], axis=0)
    probes = second_ref.shape[0]
    second_ref[...] = total[:probes]
    out_ref[...] = jnp.broadcast_to(total[probes:probes + 1], out_ref.shape)


def finish(all_ref, right_ref, image_ref, second_ref, solution_ref, residual_ref):
    right, image, second = right_ref[...], image_ref[...], second_ref[...]
    totals = jnp.sum(all_ref[...], axis=0, keepdims=True)
    lane = lax.broadcasted_iota(jnp.int32, right.shape, 1)
    row = lax.broadcasted_iota(jnp.int32, right.shape, 0)

    def moment(index):
        return jnp.sum(jnp.where(lane == row + index * right.shape[0], totals, 0.0), axis=1, keepdims=True)

    bb, bu, uu, uw = [moment(index) for index in range(4)]
    curve = bb + bu
    alpha = bb / curve
    rest = bu / curve
    norm = rest * rest * bb - 2.0 * alpha * rest * bu + alpha * alpha * uu
    lead = rest + norm / bb
    bend = (
        lead * lead * bb - 2.0 * lead * alpha * bu + alpha * alpha * uu
        + lead * (lead * bu - alpha * uu) - alpha * (lead * uu - alpha * uw)
    )
    later = norm / bend
    direction = lead * right - alpha * image
    solution_ref[...] = alpha * right + later * direction
    residual_ref[...] = right - alpha * (right + image) - later * (direction + lead * image - alpha * second)


def per_device(features, lengthscale, right_side):
    nx, nz, ncore = [lax.axis_size(axis) for axis in AXES[:3]]
    ny = lax.axis_size(COLS)
    feats, width = features.shape
    probes = right_side.shape[0]
    plane = nx * nz
    factor = float(width * plane * ncore * ny) ** (-0.5)
    block = shaped(F32, probes, width)
    swap = [(0, 1), (1, 0)]

    def exchange(values, axes):
        return lax.all_to_all(values, axes, 0, 0, tiled=True)

    def held(array):
        return pltpu.with_memory_space_constraint(array, pltpu.VMEM)

    source, given = [pltpu.with_memory_space_constraint(array, pltpu.HBM) for array in (features, right_side)]
    far_off = pl.BlockSpec(memory_space=pltpu.HBM)
    rows, right = call(
        row_copies, source, given, specs=[far_off] * 2,
        outs=[shaped(BF16, plane, feats + probes, width), pltpu.VMEM(block.shape, F32)],
        scratch=[pltpu.VMEM(features.shape, BF16), pltpu.SemaphoreType.DMA((2,))],
    )
    right = held(right)
    near = exchange(rows, ("x", "z"))
    raw = features[None]
    for axis in COLS[:2]:
        raw = lax.all_gather(raw, axis, axis=0, tiled=True)
    other = lax.ppermute(raw, COLS[2], swap)
    middle = ny // 2 * width
    held_cols = shaped(BF16, middle, feats + EXTRA)
    inverse, cols = call(columns, lengthscale.reshape(1, feats), raw, outs=[shaped(F32, feats, width), held_cols])
    near, inverse, cols = lax.optimization_barrier((near, inverse, cols))
    far = lax.ppermute(near, "core", swap)
    tile = pltpu.VMEM((middle, plane * width), BF16)
    wide = shaped(BF16, feats + EXTRA, plane * width)
    sums = shaped(F32, probes, middle)
    tile_own, sums_own, rows = call(own_near, inverse, cols, near, outs=[tile, sums, wide], limit=24)
    tile_other, sums_other, more = call(
        other_near, inverse, other, near, rows, outs=[tile, sums, held_cols], limit=24
    )
    tile_far, parts = call(
        far_product, inverse, cols, more, far, sums_own, sums_other,
        outs=[pltpu.VMEM((2 * middle, plane * width), BF16), shaped(BF16, ny, (ny + 1) * probes, width)],
        limit=24,
        scratch=[pltpu.VMEM(wide.shape, BF16), pltpu.VMEM((2 * middle, feats + EXTRA), BF16)],
    )
    parts = exchange(parts, COLS)
    image, rows = call(
        functools.partial(spread, factor), parts, outs=[block, shaped(BF16, plane, probes, width)]
    )
    both = lax.all_gather(exchange(rows, ("x", "z")), "core")
    sums = call(
        functools.partial(second_product, factor), held(tile_own), held(tile_other), held(tile_far), both, parts, right, image,
        outs=shaped(F32, ny, probes + PAD, width),
    )
    second, local = call(gathered, exchange(sums, COLS), outs=[block, shaped(F32, plane * ncore, width)])
    everyone = exchange(local, ("x", "z", "core"))
    return call(finish, everyone, right, image, second, outs=[block, block])


def solution(mesh):
    fine = Mesh(mesh.devices.reshape(4, 8, 2, 2, 2, 2), AXES)
    split = P(None, AXES)
    return jax.shard_map(
        per_device,
        mesh=fine,
        in_specs=(split, P(), split),
        out_specs=(split, split),
        check_vma=False,
    )
```

```python
import functools

import jax
import jax.numpy as jnp
from jax import lax
from jax.experimental import pallas as pl
from jax.experimental.pallas import tpu as pltpu
from jax.sharding import Mesh, PartitionSpec as P

F32, BF16 = jnp.float32, jnp.bfloat16
EXTRA = 16
PAD = 8
CHUNK = 1024
COLS = ("ya", "yb", "yc")
AXES = ("x", "z", "core") + COLS
VMEM = pl.BlockSpec(memory_space=pltpu.VMEM)


def call(kernel, *args, outs, limit=16, scratch=(), specs=None):
    return pl.pallas_call(
        kernel,
        in_specs=specs or [VMEM] * len(args),
        out_specs=jax.tree.map(lambda _: VMEM, outs),
        out_shape=outs,
        scratch_shapes=scratch,
        compiler_params=pltpu.CompilerParams(vmem_limit_bytes=limit << 20),
    )(*args)


def shaped(dtype, *shape):
    return jax.ShapeDtypeStruct(shape, dtype)


def pieces(value):
    high = value.astype(BF16).astype(F32)
    middle = (value - high).astype(BF16).astype(F32)
    return high, middle, value - high - middle


def augmented(raw, inverse, offset):
    scaled = (raw.astype(F32) * inverse).astype(BF16)
    wide = scaled.astype(F32)
    half = jnp.sum(wide * wide, axis=0, keepdims=True) * -0.5
    high, middle, low = pieces(half)
    row = lax.broadcasted_iota(jnp.int32, (EXTRA, raw.shape[1]), 0)
    below = jnp.where(row < 6, 1.0, 0.0)
    for index, part in enumerate((high, middle, low)):
        below = jnp.where(row == offset + index, part, below)
    return jnp.concatenate([scaled, below.astype(BF16)], axis=0)


def row_copies(features_ref, right_ref, rows_ref, kept_ref, held, sems):
    moves = [
        pltpu.make_async_copy(features_ref, held, sems.at[0]),
        pltpu.make_async_copy(right_ref, kept_ref, sems.at[1]),
    ]
    for move in moves:
        move.start()
    for move in moves:
        move.wait()
    features, right = held[...], kept_ref[...].astype(BF16)
    feats = features.shape[0]
    for index in range(rows_ref.shape[0]):
        rows_ref[index, :feats, :] = features
        rows_ref[index, feats:, :] = right


def columns(scale_ref, cols_ref, inverse_ref, out_ref):
    ncols, feats, width = cols_ref.shape
    lane = lax.broadcasted_iota(jnp.int32, (feats, feats), 1)
    row = lax.broadcasted_iota(jnp.int32, (feats, feats), 0)
    scale = jnp.sum(jnp.where(lane == row, scale_ref[...], 0.0), axis=1, keepdims=True)
    inverse = jnp.broadcast_to(1.0 / scale, (feats, width))
    inverse_ref[...] = inverse
    ya, yb = [lax.axis_index(axis) for axis in COLS[:2]]
    for index in range(ncols):
        first, middle, last = index // 4, index // 2 % 2, index % 2
        place = last * 4 + (1 - ya if first else ya) * 2 + (1 - yb if middle else yb)
        block = augmented(cols_ref[place], inverse, 0).astype(F32)
        out_ref[index * width:(index + 1) * width, :] = jnp.transpose(block).astype(BF16)


def dot_last(left, right):
    return lax.dot_general(left, right, (((1,), (1,)), ((), ())), preferred_element_type=F32)


def tile_and_product(inverse_ref, cols_ref, rows_ref, tile_ref, rows, add):
    feats, width = inverse_ref.shape
    inverse = inverse_ref[...]
    nrows = rows_ref.shape[0]
    for index in range(nrows):
        rows[:, index * width:(index + 1) * width] = augmented(rows_ref[index, :feats, :], inverse, 3)
    vectors = jnp.concatenate([rows_ref[index, feats:, :] for index in range(nrows)], axis=1)
    for begin in range(0, cols_ref.shape[0], CHUNK):
        inner = jnp.dot(cols_ref[begin:begin + CHUNK, :], rows[...], preferred_element_type=F32)
        tile = jnp.exp(inner).astype(BF16)
        tile_ref[begin:begin + CHUNK, :] = tile
        part = dot_last(vectors, tile)
        for index in range(CHUNK // width):
            add(begin // width + index, part[:, index * width:(index + 1) * width])


def near_product(inverse_ref, cols_ref, rows_ref, tile_ref, sums_ref, rows):
    def add(index, piece):
        sums_ref[index] = piece

    tile_and_product(inverse_ref, cols_ref, rows_ref, tile_ref, rows, add)


def far_product(inverse_ref, cols_ref, rows_ref, sums_ref, tile_ref, out_ref, rows):
    ncols, probes, _ = sums_ref.shape

    def add(index, piece):
        value = sums_ref[index] + piece
        high = value.astype(BF16)
        for peer in range(ncols):
            out_ref[peer, index * probes:(index + 1) * probes, :] = high
        out_ref[index, ncols * probes:, :] = (value - high.astype(F32)).astype(BF16)

    tile_and_product(inverse_ref, cols_ref, rows_ref, tile_ref, rows, add)


def spread(factor, parts_ref, image_ref, out_ref):
    probes = image_ref.shape[0]
    last = parts_ref.shape[1] - probes
    mine = pl.ds(pl.multiple_of(lax.axis_index(COLS) * probes, probes), probes)
    own = jnp.zeros(image_ref.shape, F32)
    for peer in range(parts_ref.shape[0]):
        own += parts_ref[peer, mine, :].astype(F32) + parts_ref[peer, last:, :].astype(F32)
    image = own * factor
    image_ref[...] = image
    small = image.astype(BF16)
    for index in range(out_ref.shape[0]):
        out_ref[index] = small


def placed(values, shape):
    lane = lax.broadcasted_iota(jnp.int32, shape, 1)
    row = lax.broadcasted_iota(jnp.int32, shape, 0)
    grid = jnp.zeros(shape, F32)
    for index, value in values:
        grid = jnp.where(lane == row + index * shape[0], value, grid)
    return jnp.sum(grid, axis=0, keepdims=True)


def second_product(factor, near_ref, far_ref, rows_ref, parts_ref, right_ref, image_ref, out_ref):
    ncols = out_ref.shape[0]
    probes, width = right_ref.shape
    me = lax.axis_index("core")
    part = jnp.zeros((probes, ncols * width), F32)
    for half, tile_ref in ((me, near_ref), (1 - me, far_ref)):
        vectors = jnp.concatenate([rows_ref[half, index] for index in range(rows_ref.shape[1])], axis=1)
        part += dot_last(vectors, tile_ref[...])
    total = jnp.zeros((probes, width), F32)
    for index in range(ncols):
        first = jnp.zeros((probes, width), F32)
        for peer in range(parts_ref.shape[0]):
            first += parts_ref[peer, index * probes:(index + 1) * probes, :].astype(F32)
        second = part[:, index * width:(index + 1) * width] * factor
        out_ref[index, :probes, :] = second
        total += first * second
    right, image = right_ref[...], image_ref[...]
    products = (right * right, right * image, image * image, total * factor)
    sums = [(index, jnp.sum(product, axis=1, keepdims=True)) for index, product in enumerate(products)]
    row = lax.broadcasted_iota(jnp.int32, (PAD, width), 0)
    scalars = jnp.where(row == 0, placed(sums, (probes, width)), 0.0)
    for index in range(ncols):
        out_ref[index, probes:, :] = scalars


def gathered(parts_ref, second_ref, out_ref):
    total = jnp.sum(parts_ref[...], axis=0)
    probes = second_ref.shape[0]
    second_ref[...] = total[:probes]
    out_ref[...] = jnp.broadcast_to(total[probes:probes + 1], out_ref.shape)


def finish(all_ref, right_ref, image_ref, second_ref, solution_ref, residual_ref):
    right, image, second = right_ref[...], image_ref[...], second_ref[...]
    totals = jnp.sum(all_ref[...], axis=0, keepdims=True)
    lane = lax.broadcasted_iota(jnp.int32, right.shape, 1)
    row = lax.broadcasted_iota(jnp.int32, right.shape, 0)

    def moment(index):
        return jnp.sum(jnp.where(lane == row + index * right.shape[0], totals, 0.0), axis=1, keepdims=True)

    bb, bu, uu, uw = [moment(index) for index in range(4)]
    curve = bb + bu
    alpha = bb / curve
    rest = bu / curve
    norm = rest * rest * bb - 2.0 * alpha * rest * bu + alpha * alpha * uu
    lead = rest + norm / bb
    bend = (
        lead * lead * bb - 2.0 * lead * alpha * bu + alpha * alpha * uu
        + lead * (lead * bu - alpha * uu) - alpha * (lead * uu - alpha * uw)
    )
    later = norm / bend
    direction = lead * right - alpha * image
    solution_ref[...] = alpha * right + later * direction
    residual_ref[...] = right - alpha * (right + image) - later * (direction + lead * image - alpha * second)


def per_device(features, lengthscale, right_side):
    nx, nz, ncore = [lax.axis_size(axis) for axis in AXES[:3]]
    ny = lax.axis_size(COLS)
    feats, width = features.shape
    probes = right_side.shape[0]
    plane = nx * nz
    factor = float(width * plane * ncore * ny) ** (-0.5)
    block = shaped(F32, probes, width)
    swap = [(0, 1), (1, 0)]

    def exchange(values, axes):
        return lax.all_to_all(values, axes, 0, 0, tiled=True)

    def held(array):
        return pltpu.with_memory_space_constraint(array, pltpu.VMEM)

    source, given = [pltpu.with_memory_space_constraint(array, pltpu.HBM) for array in (features, right_side)]
    far_off = pl.BlockSpec(memory_space=pltpu.HBM)
    rows, right = call(
        row_copies, source, given, specs=[far_off] * 2,
        outs=[shaped(BF16, plane, feats + probes, width), pltpu.VMEM(block.shape, F32)],
        scratch=[pltpu.VMEM(features.shape, BF16), pltpu.SemaphoreType.DMA((2,))],
    )
    right = held(right)
    near = exchange(rows, ("x", "z"))
    cols = jnp.stack([features] + [
        lax.ppermute(features, COLS[:2], [(index, index ^ other) for index in range(4)]) for other in (1, 2, 3)
    ])
    cols = lax.all_gather(cols, COLS[2], axis=0, tiled=True)
    inverse, cols = call(
        columns, lengthscale.reshape(1, feats), cols,
        outs=[shaped(F32, feats, width), shaped(BF16, ny * width, feats + EXTRA)],
    )
    near, inverse, cols = lax.optimization_barrier((near, inverse, cols))
    far = lax.ppermute(near, "core", swap)
    tile = pltpu.VMEM((ny * width, plane * width), BF16)
    scratch = [pltpu.VMEM((feats + EXTRA, plane * width), BF16)]
    tile_near, sums = call(
        near_product, inverse, cols, near, outs=[tile, shaped(F32, ny, probes, width)], limit=24, scratch=scratch
    )
    tile_far, parts = call(
        far_product, inverse, cols, far, sums, outs=[tile, shaped(BF16, ny, (ny + 1) * probes, width)],
        limit=24, scratch=scratch,
    )
    parts = exchange(parts, COLS)
    image, rows = call(
        functools.partial(spread, factor), parts, outs=[block, shaped(BF16, plane, probes, width)]
    )
    both = lax.all_gather(exchange(rows, ("x", "z")), "core")
    sums = call(
        functools.partial(second_product, factor), held(tile_near), held(tile_far), both, parts, right, image,
        outs=shaped(F32, ny, probes + PAD, width),
    )
    second, local = call(gathered, exchange(sums, COLS), outs=[block, shaped(F32, plane * ncore, width)])
    everyone = exchange(local, ("x", "z", "core"))
    return call(finish, everyone, right, image, second, outs=[block, block])


def solution(mesh):
    fine = Mesh(mesh.devices.reshape(4, 8, 2, 2, 2, 2), AXES)
    split = P(None, AXES)
    return jax.shard_map(
        per_device,
        mesh=fine,
        in_specs=(split, P(), split),
        out_specs=(split, split),
        check_vma=False,
    )
```

```python
import functools

import jax
import jax.numpy as jnp
from jax import lax
from jax.experimental import pallas as pl
from jax.experimental.pallas import tpu as pltpu
from jax.sharding import Mesh, PartitionSpec as P

F32, BF16 = jnp.float32, jnp.bfloat16
EXTRA = 16
PAD = 8
CHUNK = 1024
COLS = ("ya", "yb", "yc")
AXES = ("x", "z", "core") + COLS
VMEM = pl.BlockSpec(memory_space=pltpu.VMEM)


def call(kernel, *args, outs, limit=16, scratch=(), specs=None):
    return pl.pallas_call(
        kernel,
        in_specs=specs or [VMEM] * len(args),
        out_specs=jax.tree.map(lambda _: VMEM, outs),
        out_shape=outs,
        scratch_shapes=scratch,
        compiler_params=pltpu.CompilerParams(vmem_limit_bytes=limit << 20),
    )(*args)


def shaped(dtype, *shape):
    return jax.ShapeDtypeStruct(shape, dtype)


def pieces(value):
    high = value.astype(BF16).astype(F32)
    middle = (value - high).astype(BF16).astype(F32)
    return high, middle, value - high - middle


def augmented(raw, inverse, offset):
    scaled = (raw.astype(F32) * inverse).astype(BF16)
    wide = scaled.astype(F32)
    half = jnp.sum(wide * wide, axis=0, keepdims=True) * -0.5
    high, middle, low = pieces(half)
    row = lax.broadcasted_iota(jnp.int32, (EXTRA, raw.shape[1]), 0)
    below = jnp.where(row < 6, 1.0, 0.0)
    for index, part in enumerate((high, middle, low)):
        below = jnp.where(row == offset + index, part, below)
    return jnp.concatenate([scaled, below.astype(BF16)], axis=0)


def row_copies(features_ref, right_ref, scale_ref, rows_ref, kept_ref, inverse_ref, held, scales, sems):
    moves = [
        pltpu.make_async_copy(features_ref, held, sems.at[0]),
        pltpu.make_async_copy(right_ref, kept_ref, sems.at[1]),
        pltpu.make_async_copy(scale_ref, scales, sems.at[2]),
    ]
    for move in moves:
        move.start()
    for move in moves:
        move.wait()
    features, right = held[...], kept_ref[...].astype(BF16)
    feats = features.shape[0]
    for index in range(rows_ref.shape[0]):
        rows_ref[index, :feats, :] = features
        rows_ref[index, feats:, :] = right
    lane = lax.broadcasted_iota(jnp.int32, (feats, feats), 1)
    row = lax.broadcasted_iota(jnp.int32, (feats, feats), 0)
    scale = jnp.sum(jnp.where(lane == row, scales[...], 0.0), axis=1, keepdims=True)
    inverse_ref[...] = jnp.broadcast_to(1.0 / scale, inverse_ref.shape)


def columns(order, inverse_ref, cols_ref, out_ref):
    width = cols_ref.shape[2]
    for place, index in enumerate(order):
        block = augmented(cols_ref[place], inverse_ref[...], 0).astype(F32)
        out_ref[index * width:(index + 1) * width, :] = jnp.transpose(block).astype(BF16)


def dot_last(left, right):
    return lax.dot_general(left, right, (((1,), (1,)), ((), ())), preferred_element_type=F32)


def tile_and_product(inverse_ref, cols_ref, rows_ref, tile_ref, rows, add):
    feats, width = inverse_ref.shape
    inverse = inverse_ref[...]
    nrows = rows_ref.shape[0]
    for index in range(nrows):
        rows[:, index * width:(index + 1) * width] = augmented(rows_ref[index, :feats, :], inverse, 3)
    vectors = jnp.concatenate([rows_ref[index, feats:, :] for index in range(nrows)], axis=1)
    for begin in range(0, cols_ref.shape[0], CHUNK):
        inner = jnp.dot(cols_ref[begin:begin + CHUNK, :], rows[...], preferred_element_type=F32)
        tile = jnp.exp(inner).astype(BF16)
        tile_ref[begin:begin + CHUNK, :] = tile
        part = dot_last(vectors, tile)
        for index in range(CHUNK // width):
            add(begin // width + index, part[:, index * width:(index + 1) * width])


def near_product(inverse_ref, cols_ref, rows_ref, tile_ref, sums_ref, rows):
    def add(index, piece):
        sums_ref[index] = piece

    tile_and_product(inverse_ref, cols_ref, rows_ref, tile_ref, rows, add)


def far_product(inverse_ref, cols_ref, rows_ref, sums_ref, tile_ref, out_ref, rows):
    ncols, probes, _ = sums_ref.shape

    def add(index, piece):
        value = sums_ref[index] + piece
        high = value.astype(BF16)
        for peer in range(ncols):
            out_ref[peer, index * probes:(index + 1) * probes, :] = high
        out_ref[index, ncols * probes:, :] = (value - high.astype(F32)).astype(BF16)

    tile_and_product(inverse_ref, cols_ref, rows_ref, tile_ref, rows, add)


def spread(factor, parts_ref, image_ref, out_ref):
    probes = image_ref.shape[0]
    last = parts_ref.shape[1] - probes
    mine = pl.ds(pl.multiple_of(lax.axis_index(COLS) * probes, probes), probes)
    own = jnp.zeros(image_ref.shape, F32)
    for peer in range(parts_ref.shape[0]):
        own += parts_ref[peer, mine, :].astype(F32) + parts_ref[peer, last:, :].astype(F32)
    image = own * factor
    image_ref[...] = image
    small = image.astype(BF16)
    for index in range(out_ref.shape[0]):
        out_ref[index] = small


def placed(values, shape):
    lane = lax.broadcasted_iota(jnp.int32, shape, 1)
    row = lax.broadcasted_iota(jnp.int32, shape, 0)
    grid = jnp.zeros(shape, F32)
    for index, value in values:
        grid = jnp.where(lane == row + index * shape[0], value, grid)
    return jnp.sum(grid, axis=0, keepdims=True)


def second_product(factor, near_ref, far_ref, rows_ref, parts_ref, right_ref, image_ref, out_ref):
    ncols = out_ref.shape[0]
    probes, width = right_ref.shape
    me = lax.axis_index("core")
    part = jnp.zeros((probes, ncols * width), F32)
    for half, tile_ref in ((me, near_ref), (1 - me, far_ref)):
        vectors = jnp.concatenate([rows_ref[half, index] for index in range(rows_ref.shape[1])], axis=1)
        part += dot_last(vectors, tile_ref[...])
    total = jnp.zeros((probes, width), F32)
    for index in range(ncols):
        first = jnp.zeros((probes, width), F32)
        for peer in range(parts_ref.shape[0]):
            first += parts_ref[peer, index * probes:(index + 1) * probes, :].astype(F32)
        second = part[:, index * width:(index + 1) * width] * factor
        out_ref[index, :probes, :] = second
        total += first * second
    right, image = right_ref[...], image_ref[...]
    products = (right * right, right * image, image * image, total * factor)
    sums = [(index, jnp.sum(product, axis=1, keepdims=True)) for index, product in enumerate(products)]
    row = lax.broadcasted_iota(jnp.int32, (PAD, width), 0)
    scalars = jnp.where(row == 0, placed(sums, (probes, width)), 0.0)
    for index in range(ncols):
        out_ref[index, probes:, :] = scalars


def gathered(parts_ref, second_ref, out_ref):
    total = jnp.sum(parts_ref[...], axis=0)
    probes = second_ref.shape[0]
    second_ref[...] = total[:probes]
    out_ref[...] = jnp.broadcast_to(total[probes:probes + 1], out_ref.shape)


def finish(all_ref, right_ref, image_ref, second_ref, solution_ref, residual_ref):
    right, image, second = right_ref[...], image_ref[...], second_ref[...]
    totals = jnp.sum(all_ref[...], axis=0, keepdims=True)
    lane = lax.broadcasted_iota(jnp.int32, right.shape, 1)
    row = lax.broadcasted_iota(jnp.int32, right.shape, 0)

    def moment(index):
        return jnp.sum(jnp.where(lane == row + index * right.shape[0], totals, 0.0), axis=1, keepdims=True)

    bb, bu, uu, uw = [moment(index) for index in range(4)]
    curve = bb + bu
    alpha = bb / curve
    rest = bu / curve
    norm = rest * rest * bb - 2.0 * alpha * rest * bu + alpha * alpha * uu
    lead = rest + norm / bb
    bend = (
        lead * lead * bb - 2.0 * lead * alpha * bu + alpha * alpha * uu
        + lead * (lead * bu - alpha * uu) - alpha * (lead * uu - alpha * uw)
    )
    later = norm / bend
    direction = lead * right - alpha * image
    solution_ref[...] = alpha * right + later * direction
    residual_ref[...] = right - alpha * (right + image) - later * (direction + lead * image - alpha * second)


def per_device(features, lengthscale, right_side):
    nx, nz, ncore = [lax.axis_size(axis) for axis in AXES[:3]]
    ny = lax.axis_size(COLS)
    feats, width = features.shape
    probes = right_side.shape[0]
    plane = nx * nz
    factor = float(width * plane * ncore * ny) ** (-0.5)
    block = shaped(F32, probes, width)
    swap = [(0, 1), (1, 0)]

    def exchange(values, axes):
        return lax.all_to_all(values, axes, 0, 0, tiled=True)

    def held(array):
        return pltpu.with_memory_space_constraint(array, pltpu.VMEM)

    given = [
        pltpu.with_memory_space_constraint(array, pltpu.HBM)
        for array in (features, right_side, lengthscale.reshape(1, feats))
    ]
    far_off = pl.BlockSpec(memory_space=pltpu.HBM)
    rows, right, inverse = call(
        row_copies, *given, specs=[far_off] * 3,
        outs=[
            shaped(BF16, plane, feats + probes, width), pltpu.VMEM(block.shape, F32), pltpu.VMEM((feats, width), F32),
        ],
        scratch=[pltpu.VMEM(features.shape, BF16), pltpu.VMEM((1, feats), F32), pltpu.SemaphoreType.DMA((3,))],
    )
    right, inverse = held(right), held(inverse)
    near = exchange(rows, ("x", "z"))
    cols = features[None]
    for axis in COLS:
        cols = lax.all_gather(cols, axis, axis=0, tiled=True)
    order = [sum(((place >> bit) & 1) << (len(COLS) - 1 - bit) for bit in range(len(COLS))) for place in range(ny)]
    cols = call(
        functools.partial(columns, order), inverse, cols, outs=shaped(BF16, ny * width, feats + EXTRA)
    )
    near, cols = lax.optimization_barrier((near, cols))
    far = lax.ppermute(near, "core", swap)
    tile = pltpu.VMEM((ny * width, plane * width), BF16)
    scratch = [pltpu.VMEM((feats + EXTRA, plane * width), BF16)]
    tile_near, sums = call(
        near_product, inverse, cols, near, outs=[tile, shaped(F32, ny, probes, width)], limit=24, scratch=scratch
    )
    tile_far, parts = call(
        far_product, inverse, cols, far, sums, outs=[tile, shaped(BF16, ny, (ny + 1) * probes, width)],
        limit=24, scratch=scratch,
    )
    parts = exchange(parts, COLS)
    image, rows = call(
        functools.partial(spread, factor), parts, outs=[block, shaped(BF16, plane, probes, width)]
    )
    both = lax.all_gather(exchange(rows, ("x", "z")), "core")
    sums = call(
        functools.partial(second_product, factor), held(tile_near), held(tile_far), both, parts, right, image,
        outs=shaped(F32, ny, probes + PAD, width),
    )
    second, local = call(gathered, exchange(sums, COLS), outs=[block, shaped(F32, plane * ncore, width)])
    everyone = exchange(local, ("x", "z", "core"))
    return call(finish, everyone, right, image, second, outs=[block, block])


def solution(mesh):
    fine = Mesh(mesh.devices.reshape(4, 8, 2, 2, 2, 2), AXES)
    split = P(None, AXES)
    return jax.shard_map(
        per_device,
        mesh=fine,
        in_specs=(split, P(), split),
        out_specs=(split, split),
        check_vma=False,
    )
```

```python
import functools

import jax
import jax.numpy as jnp
from jax import lax
from jax.experimental import pallas as pl
from jax.experimental.pallas import tpu as pltpu
from jax.sharding import Mesh, PartitionSpec as P

F32, BF16 = jnp.float32, jnp.bfloat16
EXTRA = 16
PAD = 8
COLS = ("ya", "yb", "yc")
AXES = ("x", "z", "core") + COLS
VMEM = pl.BlockSpec(memory_space=pltpu.VMEM)


def call(kernel, *args, outs, limit=16, scratch=(), specs=None):
    return pl.pallas_call(
        kernel,
        in_specs=specs or [VMEM] * len(args),
        out_specs=jax.tree.map(lambda _: VMEM, outs),
        out_shape=outs,
        scratch_shapes=scratch,
        compiler_params=pltpu.CompilerParams(vmem_limit_bytes=limit << 20),
    )(*args)


def shaped(dtype, *shape):
    return jax.ShapeDtypeStruct(shape, dtype)


def pieces(value):
    high = value.astype(BF16).astype(F32)
    middle = (value - high).astype(BF16).astype(F32)
    return high, middle, value - high - middle


def augmented(raw, inverse, offset):
    scaled = (raw.astype(F32) * inverse).astype(BF16)
    wide = scaled.astype(F32)
    half = jnp.sum(wide * wide, axis=0, keepdims=True) * -0.5
    high, middle, low = pieces(half)
    row = lax.broadcasted_iota(jnp.int32, (EXTRA, raw.shape[1]), 0)
    below = jnp.where(row < 6, 1.0, 0.0)
    for index, part in enumerate((high, middle, low)):
        below = jnp.where(row == offset + index, part, below)
    return jnp.concatenate([scaled, below.astype(BF16)], axis=0)


def row_copies(features_ref, right_ref, scale_ref, rows_ref, kept_ref, inverse_ref, held, scales, sems):
    moves = [
        pltpu.make_async_copy(features_ref, held, sems.at[0]),
        pltpu.make_async_copy(right_ref, kept_ref, sems.at[1]),
        pltpu.make_async_copy(scale_ref, scales, sems.at[2]),
    ]
    for move in moves:
        move.start()
    for move in moves:
        move.wait()
    features, right = held[...], kept_ref[...].astype(BF16)
    feats = features.shape[0]
    for index in range(rows_ref.shape[0]):
        rows_ref[index, :feats, :] = features
        rows_ref[index, feats:, :] = right
    lane = lax.broadcasted_iota(jnp.int32, (feats, feats), 1)
    row = lax.broadcasted_iota(jnp.int32, (feats, feats), 0)
    scale = jnp.sum(jnp.where(lane == row, scales[...], 0.0), axis=1, keepdims=True)
    inverse_ref[...] = jnp.broadcast_to(1.0 / scale, inverse_ref.shape)


def put_columns(cols_ref, inverse, out_ref):
    ncols, _, width = cols_ref.shape
    for index in range(ncols):
        block = augmented(cols_ref[index % 2 * 2 + index // 2], inverse, 0).astype(F32)
        out_ref[index * width:(index + 1) * width, :] = jnp.transpose(block).astype(BF16)


def columns(inverse_ref, cols_ref, out_ref):
    put_columns(cols_ref, inverse_ref[...], out_ref)


def dot_last(left, right):
    return lax.dot_general(left, right, (((1,), (1,)), ((), ())), preferred_element_type=F32)


def put_rows(rows_ref, inverse, out_ref):
    feats, width = inverse.shape
    for index in range(rows_ref.shape[0]):
        out_ref[:, index * width:(index + 1) * width] = augmented(rows_ref[index, :feats, :], inverse, 3)


def vectors_of(rows_ref, feats):
    return jnp.concatenate([rows_ref[index, feats:, :] for index in range(rows_ref.shape[0])], axis=1)


def tile_and_product(cols_ref, rows_ref, vectors, tile_ref):
    inner = jnp.dot(cols_ref[...], rows_ref[...], preferred_element_type=F32)
    tile = jnp.exp(inner).astype(BF16)
    tile_ref[...] = tile
    return dot_last(vectors, tile)


def own_near(inverse_ref, cols_ref, near_ref, tile_ref, sums_ref, rows_ref):
    put_rows(near_ref, inverse_ref[...], rows_ref)
    sums_ref[...] = tile_and_product(cols_ref, rows_ref, vectors_of(near_ref, inverse_ref.shape[0]), tile_ref)


def other_near(inverse_ref, raw_ref, near_ref, rows_ref, tile_ref, sums_ref, cols_ref):
    put_columns(raw_ref, inverse_ref[...], cols_ref)
    sums_ref[...] = tile_and_product(cols_ref, rows_ref, vectors_of(near_ref, inverse_ref.shape[0]), tile_ref)


def placing(ncols):
    me = lax.axis_index(COLS[2])
    half = ncols // 2
    return [index % half * 2 + (me if index < half else 1 - me) for index in range(ncols)]


def far_product(inverse_ref, own_ref, other_ref, far_ref, own_sums_ref, other_sums_ref, tile_ref, out_ref, rows, cols):
    probes = own_sums_ref.shape[0]
    ncols = out_ref.shape[0]
    feats, width = inverse_ref.shape
    middle = own_ref.shape[0]
    cols[:middle, :] = own_ref[...]
    cols[middle:, :] = other_ref[...]
    put_rows(far_ref, inverse_ref[...], rows)
    part = tile_and_product(cols, rows, vectors_of(far_ref, feats), tile_ref)
    part += jnp.concatenate([own_sums_ref[...], other_sums_ref[...]], axis=1)
    for index, place in enumerate(placing(ncols)):
        value = part[:, index * width:(index + 1) * width]
        high = value.astype(BF16)
        where = pl.ds(pl.multiple_of(place * probes, probes), probes)
        for peer in range(ncols):
            out_ref[peer, where, :] = high
        out_ref[place, ncols * probes:, :] = (value - high.astype(F32)).astype(BF16)


def spread(factor, parts_ref, image_ref, out_ref):
    probes = image_ref.shape[0]
    last = parts_ref.shape[1] - probes
    mine = pl.ds(pl.multiple_of(lax.axis_index(COLS) * probes, probes), probes)
    own = jnp.zeros(image_ref.shape, F32)
    for peer in range(parts_ref.shape[0]):
        own += parts_ref[peer, mine, :].astype(F32) + parts_ref[peer, last:, :].astype(F32)
    image = own * factor
    image_ref[...] = image
    small = image.astype(BF16)
    for index in range(out_ref.shape[0]):
        out_ref[index] = small


def placed(values, shape):
    lane = lax.broadcasted_iota(jnp.int32, shape, 1)
    row = lax.broadcasted_iota(jnp.int32, shape, 0)
    grid = jnp.zeros(shape, F32)
    for index, value in values:
        grid = jnp.where(lane == row + index * shape[0], value, grid)
    return jnp.sum(grid, axis=0, keepdims=True)


def second_product(factor, own_ref, other_ref, far_ref, rows_ref, parts_ref, right_ref, image_ref, out_ref):
    ncols = out_ref.shape[0]
    probes, width = right_ref.shape
    me = lax.axis_index("core")
    near, far = [
        jnp.concatenate([rows_ref[half, index] for index in range(rows_ref.shape[1])], axis=1) for half in (me, 1 - me)
    ]
    part = dot_last(far, far_ref[...])
    part += jnp.concatenate([dot_last(near, own_ref[...]), dot_last(near, other_ref[...])], axis=1)
    total = jnp.zeros((probes, width), F32)
    for index, place in enumerate(placing(ncols)):
        where = pl.ds(pl.multiple_of(place * probes, probes), probes)
        first = jnp.zeros((probes, width), F32)
        for peer in range(parts_ref.shape[0]):
            first += parts_ref[peer, where, :].astype(F32)
        second = part[:, index * width:(index + 1) * width] * factor
        out_ref[place, :probes, :] = second
        total += first * second
    right, image = right_ref[...], image_ref[...]
    products = (right * right, right * image, image * image, total * factor)
    sums = [(index, jnp.sum(product, axis=1, keepdims=True)) for index, product in enumerate(products)]
    row = lax.broadcasted_iota(jnp.int32, (PAD, width), 0)
    scalars = jnp.where(row == 0, placed(sums, (probes, width)), 0.0)
    for index in range(ncols):
        out_ref[index, probes:, :] = scalars


def gathered(parts_ref, second_ref, out_ref):
    total = jnp.sum(parts_ref[...], axis=0)
    probes = second_ref.shape[0]
    second_ref[...] = total[:probes]
    out_ref[...] = jnp.broadcast_to(total[probes:probes + 1], out_ref.shape)


def finish(all_ref, right_ref, image_ref, second_ref, solution_ref, residual_ref):
    right, image, second = right_ref[...], image_ref[...], second_ref[...]
    totals = jnp.sum(all_ref[...], axis=0, keepdims=True)
    lane = lax.broadcasted_iota(jnp.int32, right.shape, 1)
    row = lax.broadcasted_iota(jnp.int32, right.shape, 0)

    def moment(index):
        return jnp.sum(jnp.where(lane == row + index * right.shape[0], totals, 0.0), axis=1, keepdims=True)

    bb, bu, uu, uw = [moment(index) for index in range(4)]
    curve = bb + bu
    alpha = bb / curve
    rest = bu / curve
    norm = rest * rest * bb - 2.0 * alpha * rest * bu + alpha * alpha * uu
    lead = rest + norm / bb
    bend = (
        lead * lead * bb - 2.0 * lead * alpha * bu + alpha * alpha * uu
        + lead * (lead * bu - alpha * uu) - alpha * (lead * uu - alpha * uw)
    )
    later = norm / bend
    direction = lead * right - alpha * image
    solution_ref[...] = alpha * right + later * direction
    residual_ref[...] = right - alpha * (right + image) - later * (direction + lead * image - alpha * second)


def per_device(features, lengthscale, right_side):
    nx, nz, ncore = [lax.axis_size(axis) for axis in AXES[:3]]
    ny = lax.axis_size(COLS)
    feats, width = features.shape
    probes = right_side.shape[0]
    plane = nx * nz
    factor = float(width * plane * ncore * ny) ** (-0.5)
    block = shaped(F32, probes, width)
    swap = [(0, 1), (1, 0)]

    def exchange(values, axes):
        return lax.all_to_all(values, axes, 0, 0, tiled=True)

    def held(array):
        return pltpu.with_memory_space_constraint(array, pltpu.VMEM)

    given = [
        pltpu.with_memory_space_constraint(array, pltpu.HBM)
        for array in (features, right_side, lengthscale.reshape(1, feats))
    ]
    far_off = pl.BlockSpec(memory_space=pltpu.HBM)
    rows, right, inverse = call(
        row_copies, *given, specs=[far_off] * 3,
        outs=[
            shaped(BF16, plane, feats + probes, width), pltpu.VMEM(block.shape, F32), pltpu.VMEM((feats, width), F32),
        ],
        scratch=[pltpu.VMEM(features.shape, BF16), pltpu.VMEM((1, feats), F32), pltpu.SemaphoreType.DMA((3,))],
    )
    right, inverse = held(right), held(inverse)
    near = exchange(rows, ("x", "z"))
    raw = features[None]
    for axis in COLS[:2]:
        raw = lax.all_gather(raw, axis, axis=0, tiled=True)
    other = lax.ppermute(raw, COLS[2], swap)
    middle = ny // 2 * width
    held_cols = shaped(BF16, middle, feats + EXTRA)
    cols = call(columns, inverse, raw, outs=held_cols)
    near, cols = lax.optimization_barrier((near, cols))
    far = lax.ppermute(near, "core", swap)
    tile = pltpu.VMEM((middle, plane * width), BF16)
    wide = shaped(BF16, feats + EXTRA, plane * width)
    sums = shaped(F32, probes, middle)
    tile_own, sums_own, rows = call(own_near, inverse, cols, near, outs=[tile, sums, wide], limit=24)
    tile_other, sums_other, more = call(
        other_near, inverse, other, near, rows, outs=[tile, sums, held_cols], limit=24
    )
    tile_far, parts = call(
        far_product, inverse, cols, more, far, sums_own, sums_other,
        outs=[pltpu.VMEM((2 * middle, plane * width), BF16), shaped(BF16, ny, (ny + 1) * probes, width)],
        limit=24,
        scratch=[pltpu.VMEM(wide.shape, BF16), pltpu.VMEM((2 * middle, feats + EXTRA), BF16)],
    )
    parts = exchange(parts, COLS)
    image, rows = call(
        functools.partial(spread, factor), parts, outs=[block, shaped(BF16, plane, probes, width)]
    )
    both = lax.all_gather(exchange(rows, ("x", "z")), "core")
    sums = call(
        functools.partial(second_product, factor), held(tile_own), held(tile_other), held(tile_far), both, parts, right, image,
        outs=shaped(F32, ny, probes + PAD, width),
    )
    second, local = call(gathered, exchange(sums, COLS), outs=[block, shaped(F32, plane * ncore, width)])
    everyone = exchange(local, ("x", "z", "core"))
    return call(finish, everyone, right, image, second, outs=[block, block])


def solution(mesh):
    fine = Mesh(mesh.devices.reshape(4, 8, 2, 2, 2, 2), AXES)
    split = P(None, AXES)
    return jax.shard_map(
        per_device,
        mesh=fine,
        in_specs=(split, P(), split),
        out_specs=(split, split),
        check_vma=False,
    )
```

```python
import functools

import jax
import jax.numpy as jnp
from jax import lax
from jax.experimental import pallas as pl
from jax.experimental.pallas import tpu as pltpu
from jax.sharding import Mesh, PartitionSpec as P

F32, BF16 = jnp.float32, jnp.bfloat16
EXTRA = 16
PAD = 8
COLS = ("ya", "yb", "yc")
AXES = ("x", "z", "core") + COLS
VMEM = pl.BlockSpec(memory_space=pltpu.VMEM)


def call(kernel, *args, outs, limit=16, scratch=(), specs=None):
    return pl.pallas_call(
        kernel,
        in_specs=specs or [VMEM] * len(args),
        out_specs=jax.tree.map(lambda _: VMEM, outs),
        out_shape=outs,
        scratch_shapes=scratch,
        compiler_params=pltpu.CompilerParams(vmem_limit_bytes=limit << 20),
    )(*args)


def shaped(dtype, *shape):
    return jax.ShapeDtypeStruct(shape, dtype)


def pieces(value):
    high = value.astype(BF16).astype(F32)
    middle = (value - high).astype(BF16).astype(F32)
    return high, middle, value - high - middle


def augmented(raw, inverse, offset):
    scaled = (raw.astype(F32) * inverse).astype(BF16)
    wide = scaled.astype(F32)
    half = jnp.sum(wide * wide, axis=0, keepdims=True) * -0.5
    high, middle, low = pieces(half)
    row = lax.broadcasted_iota(jnp.int32, (EXTRA, raw.shape[1]), 0)
    below = jnp.where(row < 6, 1.0, 0.0)
    for index, part in enumerate((high, middle, low)):
        below = jnp.where(row == offset + index, part, below)
    return jnp.concatenate([scaled, below.astype(BF16)], axis=0)


def row_copies(features_ref, right_ref, rows_ref, kept_ref, held, sems):
    moves = [
        pltpu.make_async_copy(features_ref, held, sems.at[0]),
        pltpu.make_async_copy(right_ref, kept_ref, sems.at[1]),
    ]
    for move in moves:
        move.start()
    for move in moves:
        move.wait()
    features, right = held[...], kept_ref[...].astype(BF16)
    feats = features.shape[0]
    for index in range(rows_ref.shape[0]):
        rows_ref[index, :feats, :] = features
        rows_ref[index, feats:, :] = right


def put_columns(cols_ref, inverse, out_ref):
    ncols, _, width = cols_ref.shape
    for index in range(ncols):
        block = augmented(cols_ref[index % 2 * 2 + index // 2], inverse, 0).astype(F32)
        out_ref[index * width:(index + 1) * width, :] = jnp.transpose(block).astype(BF16)


def columns(scale_ref, cols_ref, inverse_ref, out_ref):
    _, feats, width = cols_ref.shape
    lane = lax.broadcasted_iota(jnp.int32, (feats, feats), 1)
    row = lax.broadcasted_iota(jnp.int32, (feats, feats), 0)
    scale = jnp.sum(jnp.where(lane == row, scale_ref[...], 0.0), axis=1, keepdims=True)
    inverse = jnp.broadcast_to(1.0 / scale, (feats, width))
    inverse_ref[...] = inverse
    put_columns(cols_ref, inverse, out_ref)


def dot_last(left, right):
    return lax.dot_general(left, right, (((1,), (1,)), ((), ())), preferred_element_type=F32)


def put_rows(rows_ref, inverse, out_ref):
    feats, width = inverse.shape
    for index in range(rows_ref.shape[0]):
        out_ref[:, index * width:(index + 1) * width] = augmented(rows_ref[index, :feats, :], inverse, 3)


def vectors_of(rows_ref, feats):
    return jnp.concatenate([rows_ref[index, feats:, :] for index in range(rows_ref.shape[0])], axis=1)


def tile_and_product(cols_ref, rows_ref, vectors, tile_ref):
    inner = jnp.dot(cols_ref[...], rows_ref[...], preferred_element_type=F32)
    tile = jnp.exp(inner).astype(BF16)
    tile_ref[...] = tile
    return dot_last(vectors, tile)


def own_near(inverse_ref, cols_ref, near_ref, tile_ref, sums_ref, rows_ref):
    put_rows(near_ref, inverse_ref[...], rows_ref)
    sums_ref[...] = tile_and_product(cols_ref, rows_ref, vectors_of(near_ref, inverse_ref.shape[0]), tile_ref)


def other_near(inverse_ref, raw_ref, near_ref, rows_ref, tile_ref, sums_ref, cols_ref):
    put_columns(raw_ref, inverse_ref[...], cols_ref)
    sums_ref[...] = tile_and_product(cols_ref, rows_ref, vectors_of(near_ref, inverse_ref.shape[0]), tile_ref)


def placing(ncols):
    me = lax.axis_index(COLS[2])
    half = ncols // 2
    return [index % half * 2 + (me if index < half else 1 - me) for index in range(ncols)]


def far_product(inverse_ref, own_ref, other_ref, far_ref, own_sums_ref, other_sums_ref, tile_ref, out_ref, rows, cols):
    probes = own_sums_ref.shape[0]
    ncols = out_ref.shape[0]
    feats, width = inverse_ref.shape
    middle = own_ref.shape[0]
    cols[:middle, :] = own_ref[...]
    cols[middle:, :] = other_ref[...]
    put_rows(far_ref, inverse_ref[...], rows)
    part = tile_and_product(cols, rows, vectors_of(far_ref, feats), tile_ref)
    part += jnp.concatenate([own_sums_ref[...], other_sums_ref[...]], axis=1)
    for index, place in enumerate(placing(ncols)):
        value = part[:, index * width:(index + 1) * width]
        high = value.astype(BF16)
        where = pl.ds(pl.multiple_of(place * probes, probes), probes)
        for peer in range(ncols):
            out_ref[peer, where, :] = high
        out_ref[place, ncols * probes:, :] = (value - high.astype(F32)).astype(BF16)


def spread(factor, parts_ref, image_ref, out_ref):
    probes = image_ref.shape[0]
    last = parts_ref.shape[1] - probes
    mine = pl.ds(pl.multiple_of(lax.axis_index(COLS) * probes, probes), probes)
    own = jnp.zeros(image_ref.shape, F32)
    for peer in range(parts_ref.shape[0]):
        own += parts_ref[peer, mine, :].astype(F32) + parts_ref[peer, last:, :].astype(F32)
    image = own * factor
    image_ref[...] = image
    small = image.astype(BF16)
    for index in range(out_ref.shape[0]):
        out_ref[index] = small


def placed(values, shape):
    lane = lax.broadcasted_iota(jnp.int32, shape, 1)
    row = lax.broadcasted_iota(jnp.int32, shape, 0)
    grid = jnp.zeros(shape, F32)
    for index, value in values:
        grid = jnp.where(lane == row + index * shape[0], value, grid)
    return jnp.sum(grid, axis=0, keepdims=True)


def second_product(factor, own_ref, other_ref, far_ref, rows_ref, parts_ref, right_ref, image_ref, out_ref):
    ncols = out_ref.shape[0]
    probes, width = right_ref.shape
    me = lax.axis_index("core")
    near, far = [
        jnp.concatenate([rows_ref[index + half] for index in range(0, rows_ref.shape[0], 2)], axis=1) for half in (me, 1 - me)
    ]
    part = dot_last(far, far_ref[...])
    part += jnp.concatenate([dot_last(near, own_ref[...]), dot_last(near, other_ref[...])], axis=1)
    total = jnp.zeros((probes, width), F32)
    for index, place in enumerate(placing(ncols)):
        where = pl.ds(pl.multiple_of(place * probes, probes), probes)
        first = jnp.zeros((probes, width), F32)
        for peer in range(parts_ref.shape[0]):
            first += parts_ref[peer, where, :].astype(F32)
        second = part[:, index * width:(index + 1) * width] * factor
        out_ref[place, :probes, :] = second
        total += first * second
    right, image = right_ref[...], image_ref[...]
    products = (right * right, right * image, image * image, total * factor)
    sums = [(index, jnp.sum(product, axis=1, keepdims=True)) for index, product in enumerate(products)]
    row = lax.broadcasted_iota(jnp.int32, (PAD, width), 0)
    scalars = jnp.where(row == 0, placed(sums, (probes, width)), 0.0)
    for index in range(ncols):
        out_ref[index, probes:, :] = scalars


def gathered(parts_ref, second_ref, out_ref):
    total = jnp.sum(parts_ref[...], axis=0)
    probes = second_ref.shape[0]
    second_ref[...] = total[:probes]
    out_ref[...] = jnp.broadcast_to(total[probes:probes + 1], out_ref.shape)


def finish(all_ref, right_ref, image_ref, second_ref, solution_ref, residual_ref):
    right, image, second = right_ref[...], image_ref[...], second_ref[...]
    totals = jnp.sum(all_ref[...], axis=0, keepdims=True)
    lane = lax.broadcasted_iota(jnp.int32, right.shape, 1)
    row = lax.broadcasted_iota(jnp.int32, right.shape, 0)

    def moment(index):
        return jnp.sum(jnp.where(lane == row + index * right.shape[0], totals, 0.0), axis=1, keepdims=True)

    bb, bu, uu, uw = [moment(index) for index in range(4)]
    curve = bb + bu
    alpha = bb / curve
    rest = bu / curve
    norm = rest * rest * bb - 2.0 * alpha * rest * bu + alpha * alpha * uu
    lead = rest + norm / bb
    bend = (
        lead * lead * bb - 2.0 * lead * alpha * bu + alpha * alpha * uu
        + lead * (lead * bu - alpha * uu) - alpha * (lead * uu - alpha * uw)
    )
    later = norm / bend
    direction = lead * right - alpha * image
    solution_ref[...] = alpha * right + later * direction
    residual_ref[...] = right - alpha * (right + image) - later * (direction + lead * image - alpha * second)


def per_device(features, lengthscale, right_side):
    nx, nz, ncore = [lax.axis_size(axis) for axis in AXES[:3]]
    ny = lax.axis_size(COLS)
    feats, width = features.shape
    probes = right_side.shape[0]
    plane = nx * nz
    factor = float(width * plane * ncore * ny) ** (-0.5)
    block = shaped(F32, probes, width)
    swap = [(0, 1), (1, 0)]

    def exchange(values, axes):
        return lax.all_to_all(values, axes, 0, 0, tiled=True)

    def held(array):
        return pltpu.with_memory_space_constraint(array, pltpu.VMEM)

    source, given = [pltpu.with_memory_space_constraint(array, pltpu.HBM) for array in (features, right_side)]
    far_off = pl.BlockSpec(memory_space=pltpu.HBM)
    rows, right = call(
        row_copies, source, given, specs=[far_off] * 2,
        outs=[shaped(BF16, plane, feats + probes, width), pltpu.VMEM(block.shape, F32)],
        scratch=[pltpu.VMEM(features.shape, BF16), pltpu.SemaphoreType.DMA((2,))],
    )
    right = held(right)
    near = exchange(rows, ("x", "z"))
    raw = features[None]
    for axis in COLS[:2]:
        raw = lax.all_gather(raw, axis, axis=0, tiled=True)
    other = lax.ppermute(raw, COLS[2], swap)
    middle = ny // 2 * width
    held_cols = shaped(BF16, middle, feats + EXTRA)
    inverse, cols = call(columns, lengthscale.reshape(1, feats), raw, outs=[shaped(F32, feats, width), held_cols])
    near, inverse, cols = lax.optimization_barrier((near, inverse, cols))
    far = lax.ppermute(near, "core", swap)
    tile = pltpu.VMEM((middle, plane * width), BF16)
    wide = shaped(BF16, feats + EXTRA, plane * width)
    sums = shaped(F32, probes, middle)
    tile_own, sums_own, rows = call(own_near, inverse, cols, near, outs=[tile, sums, wide], limit=24)
    tile_other, sums_other, more = call(
        other_near, inverse, other, near, rows, outs=[tile, sums, held_cols], limit=24
    )
    tile_far, parts = call(
        far_product, inverse, cols, more, far, sums_own, sums_other,
        outs=[pltpu.VMEM((2 * middle, plane * width), BF16), shaped(BF16, ny, (ny + 1) * probes, width)],
        limit=24,
        scratch=[pltpu.VMEM(wide.shape, BF16), pltpu.VMEM((2 * middle, feats + EXTRA), BF16)],
    )
    parts = exchange(parts, COLS)
    image, rows = call(
        functools.partial(spread, factor), parts, outs=[block, shaped(BF16, plane * ncore, probes, width)]
    )
    both = exchange(rows, ("x", "z", "core"))
    sums = call(
        functools.partial(second_product, factor), held(tile_own), held(tile_other), held(tile_far), both, parts, right, image,
        outs=shaped(F32, ny, probes + PAD, width),
    )
    second, local = call(gathered, exchange(sums, COLS), outs=[block, shaped(F32, plane * ncore, width)])
    everyone = exchange(local, ("x", "z", "core"))
    return call(finish, everyone, right, image, second, outs=[block, block])


def solution(mesh):
    fine = Mesh(mesh.devices.reshape(4, 8, 2, 2, 2, 2), AXES)
    split = P(None, AXES)
    return jax.shard_map(
        per_device,
        mesh=fine,
        in_specs=(split, P(), split),
        out_specs=(split, split),
        check_vma=False,
    )
```

```python
import functools

import jax
import jax.numpy as jnp
from jax import lax
from jax.experimental import pallas as pl
from jax.experimental.pallas import tpu as pltpu
from jax.sharding import Mesh, PartitionSpec as P

F32, BF16 = jnp.float32, jnp.bfloat16
EXTRA = 16
PAD = 8
COLS = ("ya", "yb", "yc")
AXES = ("x", "z", "core") + COLS
VMEM = pl.BlockSpec(memory_space=pltpu.VMEM)


def call(kernel, *args, outs, limit=16, scratch=(), specs=None):
    return pl.pallas_call(
        kernel,
        in_specs=specs or [VMEM] * len(args),
        out_specs=jax.tree.map(lambda _: VMEM, outs),
        out_shape=outs,
        scratch_shapes=scratch,
        compiler_params=pltpu.CompilerParams(vmem_limit_bytes=limit << 20),
    )(*args)


def shaped(dtype, *shape):
    return jax.ShapeDtypeStruct(shape, dtype)


def pieces(value):
    high = value.astype(BF16).astype(F32)
    middle = (value - high).astype(BF16).astype(F32)
    return high, middle, value - high - middle


def augmented(raw, inverse, offset):
    scaled = (raw.astype(F32) * inverse).astype(BF16)
    wide = scaled.astype(F32)
    half = jnp.sum(wide * wide, axis=0, keepdims=True) * -0.5
    high, middle, low = pieces(half)
    row = lax.broadcasted_iota(jnp.int32, (EXTRA, raw.shape[1]), 0)
    below = jnp.where(row < 6, 1.0, 0.0)
    for index, part in enumerate((high, middle, low)):
        below = jnp.where(row == offset + index, part, below)
    return jnp.concatenate([scaled, below.astype(BF16)], axis=0)


def row_copies(features_ref, right_ref, scale_ref, rows_ref, kept_ref, inverse_ref, held, scales, sems):
    moves = [
        pltpu.make_async_copy(features_ref, held, sems.at[0]),
        pltpu.make_async_copy(right_ref, kept_ref, sems.at[1]),
        pltpu.make_async_copy(scale_ref, scales, sems.at[2]),
    ]
    for move in moves:
        move.start()
    for move in moves:
        move.wait()
    features, right = held[...], kept_ref[...].astype(BF16)
    feats = features.shape[0]
    for index in range(rows_ref.shape[0]):
        rows_ref[index, :feats, :] = features
        rows_ref[index, feats:, :] = right
    lane = lax.broadcasted_iota(jnp.int32, (feats, feats), 1)
    row = lax.broadcasted_iota(jnp.int32, (feats, feats), 0)
    scale = jnp.sum(jnp.where(lane == row, scales[...], 0.0), axis=1, keepdims=True)
    inverse_ref[...] = jnp.broadcast_to(1.0 / scale, inverse_ref.shape)


def put_columns(cols_ref, inverse, out_ref):
    ncols, _, width = cols_ref.shape
    for index in range(ncols):
        block = augmented(cols_ref[index % 2 * 2 + index // 2], inverse, 0).astype(F32)
        out_ref[index * width:(index + 1) * width, :] = jnp.transpose(block).astype(BF16)


def columns(inverse_ref, cols_ref, out_ref):
    put_columns(cols_ref, inverse_ref[...], out_ref)


def dot_last(left, right):
    return lax.dot_general(left, right, (((1,), (1,)), ((), ())), preferred_element_type=F32)


def put_rows(rows_ref, inverse, out_ref):
    feats, width = inverse.shape
    for index in range(rows_ref.shape[0]):
        out_ref[:, index * width:(index + 1) * width] = augmented(rows_ref[index, :feats, :], inverse, 3)


def vectors_of(rows_ref, feats):
    return jnp.concatenate([rows_ref[index, feats:, :] for index in range(rows_ref.shape[0])], axis=1)


def tile_and_product(cols_ref, rows_ref, vectors, tile_ref):
    inner = jnp.dot(cols_ref[...], rows_ref[...], preferred_element_type=F32)
    tile = jnp.exp(inner).astype(BF16)
    tile_ref[...] = tile
    return dot_last(vectors, tile)


def own_half(inverse_ref, cols_ref, rows_in_ref, tile_ref, sums_ref, rows_ref):
    put_rows(rows_in_ref, inverse_ref[...], rows_ref)
    sums_ref[...] = tile_and_product(cols_ref, rows_ref, vectors_of(rows_in_ref, inverse_ref.shape[0]), tile_ref)


def placing(ncols):
    me = lax.axis_index(COLS[2])
    half = ncols // 2
    return [index % half * 2 + (me if index < half else 1 - me) for index in range(ncols)]


def other_half(
    inverse_ref, raw_ref, near_ref, far_ref, near_rows_ref, far_rows_ref, near_sums_ref, far_sums_ref,
    near_tile_ref, far_tile_ref, out_ref, cols,
):
    probes = near_sums_ref.shape[0]
    ncols = out_ref.shape[0]
    feats, width = inverse_ref.shape
    put_columns(raw_ref, inverse_ref[...], cols)
    own = near_sums_ref[...] + far_sums_ref[...]
    other = tile_and_product(cols, near_rows_ref, vectors_of(near_ref, feats), near_tile_ref)
    other += tile_and_product(cols, far_rows_ref, vectors_of(far_ref, feats), far_tile_ref)
    part = jnp.concatenate([own, other], axis=1)
    for index, place in enumerate(placing(ncols)):
        value = part[:, index * width:(index + 1) * width]
        high = value.astype(BF16)
        where = pl.ds(pl.multiple_of(place * probes, probes), probes)
        for peer in range(ncols):
            out_ref[peer, where, :] = high
        out_ref[place, ncols * probes:, :] = (value - high.astype(F32)).astype(BF16)


def spread(factor, parts_ref, image_ref, out_ref):
    probes = image_ref.shape[0]
    last = parts_ref.shape[1] - probes
    mine = pl.ds(pl.multiple_of(lax.axis_index(COLS) * probes, probes), probes)
    own = jnp.zeros(image_ref.shape, F32)
    for peer in range(parts_ref.shape[0]):
        own += parts_ref[peer, mine, :].astype(F32) + parts_ref[peer, last:, :].astype(F32)
    image = own * factor
    image_ref[...] = image
    small = image.astype(BF16)
    for index in range(out_ref.shape[0]):
        out_ref[index] = small


def placed(values, shape):
    lane = lax.broadcasted_iota(jnp.int32, shape, 1)
    row = lax.broadcasted_iota(jnp.int32, shape, 0)
    grid = jnp.zeros(shape, F32)
    for index, value in values:
        grid = jnp.where(lane == row + index * shape[0], value, grid)
    return jnp.sum(grid, axis=0, keepdims=True)


def second_product(factor, own_ref, own_far_ref, other_ref, other_far_ref, rows_ref, parts_ref, right_ref, image_ref, out_ref):
    ncols = out_ref.shape[0]
    probes, width = right_ref.shape
    me = lax.axis_index("core")
    near, far = [
        jnp.concatenate([rows_ref[half, index] for index in range(rows_ref.shape[1])], axis=1) for half in (me, 1 - me)
    ]
    part = jnp.concatenate([
        dot_last(near, own_ref[...]) + dot_last(far, own_far_ref[...]),
        dot_last(near, other_ref[...]) + dot_last(far, other_far_ref[...]),
    ], axis=1)
    total = jnp.zeros((probes, width), F32)
    for index, place in enumerate(placing(ncols)):
        where = pl.ds(pl.multiple_of(place * probes, probes), probes)
        first = jnp.zeros((probes, width), F32)
        for peer in range(parts_ref.shape[0]):
            first += parts_ref[peer, where, :].astype(F32)
        second = part[:, index * width:(index + 1) * width] * factor
        out_ref[place, :probes, :] = second
        total += first * second
    right, image = right_ref[...], image_ref[...]
    products = (right * right, right * image, image * image, total * factor)
    sums = [(index, jnp.sum(product, axis=1, keepdims=True)) for index, product in enumerate(products)]
    row = lax.broadcasted_iota(jnp.int32, (PAD, width), 0)
    scalars = jnp.where(row == 0, placed(sums, (probes, width)), 0.0)
    for index in range(ncols):
        out_ref[index, probes:, :] = scalars


def gathered(parts_ref, second_ref, out_ref):
    total = jnp.sum(parts_ref[...], axis=0)
    probes = second_ref.shape[0]
    second_ref[...] = total[:probes]
    out_ref[...] = jnp.broadcast_to(total[probes:probes + 1], out_ref.shape)


def finish(all_ref, right_ref, image_ref, second_ref, solution_ref, residual_ref):
    right, image, second = right_ref[...], image_ref[...], second_ref[...]
    totals = jnp.sum(all_ref[...], axis=0, keepdims=True)
    lane = lax.broadcasted_iota(jnp.int32, right.shape, 1)
    row = lax.broadcasted_iota(jnp.int32, right.shape, 0)

    def moment(index):
        return jnp.sum(jnp.where(lane == row + index * right.shape[0], totals, 0.0), axis=1, keepdims=True)

    bb, bu, uu, uw = [moment(index) for index in range(4)]
    curve = bb + bu
    alpha = bb / curve
    rest = bu / curve
    norm = rest * rest * bb - 2.0 * alpha * rest * bu + alpha * alpha * uu
    lead = rest + norm / bb
    bend = (
        lead * lead * bb - 2.0 * lead * alpha * bu + alpha * alpha * uu
        + lead * (lead * bu - alpha * uu) - alpha * (lead * uu - alpha * uw)
    )
    later = norm / bend
    direction = lead * right - alpha * image
    solution_ref[...] = alpha * right + later * direction
    residual_ref[...] = right - alpha * (right + image) - later * (direction + lead * image - alpha * second)


def per_device(features, lengthscale, right_side):
    nx, nz, ncore = [lax.axis_size(axis) for axis in AXES[:3]]
    ny = lax.axis_size(COLS)
    feats, width = features.shape
    probes = right_side.shape[0]
    plane = nx * nz
    factor = float(width * plane * ncore * ny) ** (-0.5)
    block = shaped(F32, probes, width)
    swap = [(0, 1), (1, 0)]

    def exchange(values, axes):
        return lax.all_to_all(values, axes, 0, 0, tiled=True)

    def held(array):
        return pltpu.with_memory_space_constraint(array, pltpu.VMEM)

    given = [
        pltpu.with_memory_space_constraint(array, pltpu.HBM)
        for array in (features, right_side, lengthscale.reshape(1, feats))
    ]
    far_off = pl.BlockSpec(memory_space=pltpu.HBM)
    rows, right, inverse = call(
        row_copies, *given, specs=[far_off] * 3,
        outs=[
            shaped(BF16, plane, feats + probes, width), pltpu.VMEM(block.shape, F32), pltpu.VMEM((feats, width), F32),
        ],
        scratch=[pltpu.VMEM(features.shape, BF16), pltpu.VMEM((1, feats), F32), pltpu.SemaphoreType.DMA((3,))],
    )
    right, inverse = held(right), held(inverse)
    near = exchange(rows, ("x", "z"))
    raw = features[None]
    for axis in COLS[:2]:
        raw = lax.all_gather(raw, axis, axis=0, tiled=True)
    other = lax.ppermute(raw, COLS[2], swap)
    middle = ny // 2 * width
    held_cols = shaped(BF16, middle, feats + EXTRA)
    cols = call(columns, inverse, raw, outs=held_cols)
    near, cols = lax.optimization_barrier((near, cols))
    far = lax.ppermute(near, "core", swap)
    tile = pltpu.VMEM((middle, plane * width), BF16)
    wide = shaped(BF16, feats + EXTRA, plane * width)
    sums = shaped(F32, probes, middle)
    tile_own, sums_near, rows_near = call(own_half, inverse, cols, near, outs=[tile, sums, wide], limit=24)
    tile_own_far, sums_far, rows_far = call(own_half, inverse, cols, far, outs=[tile, sums, wide], limit=24)
    tile_other, tile_other_far, parts = call(
        other_half, inverse, other, near, far, rows_near, rows_far, sums_near, sums_far,
        outs=[tile, tile, shaped(BF16, ny, (ny + 1) * probes, width)],
        limit=24,
        scratch=[pltpu.VMEM((middle, feats + EXTRA), BF16)],
    )
    parts = exchange(parts, COLS)
    image, rows = call(
        functools.partial(spread, factor), parts, outs=[block, shaped(BF16, plane, probes, width)]
    )
    both = lax.all_gather(exchange(rows, ("x", "z")), "core")
    sums = call(
        functools.partial(second_product, factor), held(tile_own), held(tile_own_far), held(tile_other), held(tile_other_far), both, parts, right, image,
        outs=shaped(F32, ny, probes + PAD, width),
    )
    second, local = call(gathered, exchange(sums, COLS), outs=[block, shaped(F32, plane * ncore, width)])
    everyone = exchange(local, ("x", "z", "core"))
    return call(finish, everyone, right, image, second, outs=[block, block])


def solution(mesh):
    fine = Mesh(mesh.devices.reshape(4, 8, 2, 2, 2, 2), AXES)
    split = P(None, AXES)
    return jax.shard_map(
        per_device,
        mesh=fine,
        in_specs=(split, P(), split),
        out_specs=(split, split),
        check_vma=False,
    )
```

```python
import functools

import jax
import jax.numpy as jnp
from jax import lax
from jax.experimental import pallas as pl
from jax.experimental.pallas import tpu as pltpu
from jax.sharding import Mesh, PartitionSpec as P

F32, BF16 = jnp.float32, jnp.bfloat16
EXTRA = 16
PAD = 8
COLS = ("ya", "yb", "yc")
AXES = ("x", "z", "core") + COLS
VMEM = pl.BlockSpec(memory_space=pltpu.VMEM)


def call(kernel, *args, outs, limit=16, scratch=(), specs=None, out_specs=None):
    return pl.pallas_call(
        kernel,
        in_specs=specs or [VMEM] * len(args),
        out_specs=out_specs or jax.tree.map(lambda _: VMEM, outs),
        out_shape=outs,
        scratch_shapes=scratch,
        compiler_params=pltpu.CompilerParams(vmem_limit_bytes=limit << 20),
    )(*args)


def shaped(dtype, *shape):
    return jax.ShapeDtypeStruct(shape, dtype)


def pieces(value):
    high = value.astype(BF16).astype(F32)
    middle = (value - high).astype(BF16).astype(F32)
    return high, middle, value - high - middle


def augmented(raw, inverse, offset):
    scaled = (raw.astype(F32) * inverse).astype(BF16)
    wide = scaled.astype(F32)
    half = jnp.sum(wide * wide, axis=0, keepdims=True) * -0.5
    high, middle, low = pieces(half)
    row = lax.broadcasted_iota(jnp.int32, (EXTRA, raw.shape[1]), 0)
    below = jnp.where(row < 6, 1.0, 0.0)
    for index, part in enumerate((high, middle, low)):
        below = jnp.where(row == offset + index, part, below)
    return jnp.concatenate([scaled, below.astype(BF16)], axis=0)


def row_copies(features_ref, right_ref, scale_ref, rows_ref, kept_ref, inverse_ref, held, scales, sems, packed, out_sems):
    moves = [
        pltpu.make_async_copy(features_ref, held, sems.at[0]),
        pltpu.make_async_copy(right_ref, kept_ref, sems.at[1]),
        pltpu.make_async_copy(scale_ref, scales, sems.at[2]),
    ]
    for move in moves:
        move.start()
    for move in moves:
        move.wait()
    feats = held.shape[0]
    packed[:feats, :] = held[...]
    packed[feats:, :] = kept_ref[...].astype(BF16)
    sent = [
        pltpu.make_async_copy(packed, rows_ref.at[index], out_sems.at[index]) for index in range(rows_ref.shape[0])
    ]
    for move in sent:
        move.start()
    lane = lax.broadcasted_iota(jnp.int32, (feats, feats), 1)
    row = lax.broadcasted_iota(jnp.int32, (feats, feats), 0)
    scale = jnp.sum(jnp.where(lane == row, scales[...], 0.0), axis=1, keepdims=True)
    inverse_ref[...] = jnp.broadcast_to(1.0 / scale, inverse_ref.shape)
    for move in sent:
        move.wait()


def put_columns(cols_ref, inverse, out_ref):
    ncols, _, width = cols_ref.shape
    for index in range(ncols):
        block = augmented(cols_ref[index % 2 * 2 + index // 2], inverse, 0).astype(F32)
        out_ref[index * width:(index + 1) * width, :] = jnp.transpose(block).astype(BF16)


def columns(inverse_ref, cols_ref, out_ref):
    put_columns(cols_ref, inverse_ref[...], out_ref)


def dot_last(left, right):
    return lax.dot_general(left, right, (((1,), (1,)), ((), ())), preferred_element_type=F32)


def put_rows(rows_ref, inverse, out_ref):
    feats, width = inverse.shape
    for index in range(rows_ref.shape[0]):
        out_ref[:, index * width:(index + 1) * width] = augmented(rows_ref[index, :feats, :], inverse, 3)


def vectors_of(rows_ref, feats):
    return jnp.concatenate([rows_ref[index, feats:, :] for index in range(rows_ref.shape[0])], axis=1)


def tile_and_product(cols_ref, rows_ref, vectors, tile_ref):
    inner = jnp.dot(cols_ref[...], rows_ref[...], preferred_element_type=F32)
    tile = jnp.exp(inner).astype(BF16)
    tile_ref[...] = tile
    return dot_last(vectors, tile)


def own_half(inverse_ref, cols_ref, rows_in_ref, tile_ref, sums_ref, rows_ref):
    put_rows(rows_in_ref, inverse_ref[...], rows_ref)
    sums_ref[...] = tile_and_product(cols_ref, rows_ref, vectors_of(rows_in_ref, inverse_ref.shape[0]), tile_ref)


def placing(ncols):
    me = lax.axis_index(COLS[2])
    half = ncols // 2
    return [index % half * 2 + (me if index < half else 1 - me) for index in range(ncols)]


def other_half(
    inverse_ref, raw_ref, near_ref, far_ref, near_rows_ref, far_rows_ref, near_sums_ref, far_sums_ref,
    near_tile_ref, far_tile_ref, out_ref, cols,
):
    probes = near_sums_ref.shape[0]
    ncols = out_ref.shape[0]
    feats, width = inverse_ref.shape
    put_columns(raw_ref, inverse_ref[...], cols)
    own = near_sums_ref[...] + far_sums_ref[...]
    other = tile_and_product(cols, near_rows_ref, vectors_of(near_ref, feats), near_tile_ref)
    other += tile_and_product(cols, far_rows_ref, vectors_of(far_ref, feats), far_tile_ref)
    part = jnp.concatenate([own, other], axis=1)
    for index, place in enumerate(placing(ncols)):
        value = part[:, index * width:(index + 1) * width]
        high = value.astype(BF16)
        where = pl.ds(pl.multiple_of(place * probes, probes), probes)
        for peer in range(ncols):
            out_ref[peer, where, :] = high
        out_ref[place, ncols * probes:, :] = (value - high.astype(F32)).astype(BF16)


def spread(factor, parts_ref, image_ref, out_ref):
    probes = image_ref.shape[0]
    last = parts_ref.shape[1] - probes
    mine = pl.ds(pl.multiple_of(lax.axis_index(COLS) * probes, probes), probes)
    own = jnp.zeros(image_ref.shape, F32)
    for peer in range(parts_ref.shape[0]):
        own += parts_ref[peer, mine, :].astype(F32) + parts_ref[peer, last:, :].astype(F32)
    image = own * factor
    image_ref[...] = image
    small = image.astype(BF16)
    for index in range(out_ref.shape[0]):
        out_ref[index] = small


def placed(values, shape):
    lane = lax.broadcasted_iota(jnp.int32, shape, 1)
    row = lax.broadcasted_iota(jnp.int32, shape, 0)
    grid = jnp.zeros(shape, F32)
    for index, value in values:
        grid = jnp.where(lane == row + index * shape[0], value, grid)
    return jnp.sum(grid, axis=0, keepdims=True)


def second_product(factor, own_ref, own_far_ref, other_ref, other_far_ref, rows_ref, parts_ref, right_ref, image_ref, out_ref):
    ncols = out_ref.shape[0]
    probes, width = right_ref.shape
    me = lax.axis_index("core")
    near, far = [
        jnp.concatenate([rows_ref[half, index] for index in range(rows_ref.shape[1])], axis=1) for half in (me, 1 - me)
    ]
    part = jnp.concatenate([
        dot_last(near, own_ref[...]) + dot_last(far, own_far_ref[...]),
        dot_last(near, other_ref[...]) + dot_last(far, other_far_ref[...]),
    ], axis=1)
    total = jnp.zeros((probes, width), F32)
    for index, place in enumerate(placing(ncols)):
        where = pl.ds(pl.multiple_of(place * probes, probes), probes)
        first = jnp.zeros((probes, width), F32)
        for peer in range(parts_ref.shape[0]):
            first += parts_ref[peer, where, :].astype(F32)
        second = part[:, index * width:(index + 1) * width] * factor
        out_ref[place, :probes, :] = second
        total += first * second
    right, image = right_ref[...], image_ref[...]
    products = (right * right, right * image, image * image, total * factor)
    sums = [(index, jnp.sum(product, axis=1, keepdims=True)) for index, product in enumerate(products)]
    row = lax.broadcasted_iota(jnp.int32, (PAD, width), 0)
    scalars = jnp.where(row == 0, placed(sums, (probes, width)), 0.0)
    for index in range(ncols):
        out_ref[index, probes:, :] = scalars


def gathered(parts_ref, second_ref, out_ref):
    total = jnp.sum(parts_ref[...], axis=0)
    probes = second_ref.shape[0]
    second_ref[...] = total[:probes]
    out_ref[...] = jnp.broadcast_to(total[probes:probes + 1], out_ref.shape)


def finish(all_ref, right_ref, image_ref, second_ref, solution_ref, residual_ref):
    right, image, second = right_ref[...], image_ref[...], second_ref[...]
    totals = jnp.sum(all_ref[...], axis=0, keepdims=True)
    lane = lax.broadcasted_iota(jnp.int32, right.shape, 1)
    row = lax.broadcasted_iota(jnp.int32, right.shape, 0)

    def moment(index):
        return jnp.sum(jnp.where(lane == row + index * right.shape[0], totals, 0.0), axis=1, keepdims=True)

    bb, bu, uu, uw = [moment(index) for index in range(4)]
    curve = bb + bu
    alpha = bb / curve
    rest = bu / curve
    norm = rest * rest * bb - 2.0 * alpha * rest * bu + alpha * alpha * uu
    lead = rest + norm / bb
    bend = (
        lead * lead * bb - 2.0 * lead * alpha * bu + alpha * alpha * uu
        + lead * (lead * bu - alpha * uu) - alpha * (lead * uu - alpha * uw)
    )
    later = norm / bend
    direction = lead * right - alpha * image
    solution_ref[...] = alpha * right + later * direction
    residual_ref[...] = right - alpha * (right + image) - later * (direction + lead * image - alpha * second)


def per_device(features, lengthscale, right_side):
    nx, nz, ncore = [lax.axis_size(axis) for axis in AXES[:3]]
    ny = lax.axis_size(COLS)
    feats, width = features.shape
    probes = right_side.shape[0]
    plane = nx * nz
    factor = float(width * plane * ncore * ny) ** (-0.5)
    block = shaped(F32, probes, width)
    swap = [(0, 1), (1, 0)]

    def exchange(values, axes):
        return lax.all_to_all(values, axes, 0, 0, tiled=True)

    def held(array):
        return pltpu.with_memory_space_constraint(array, pltpu.VMEM)

    given = [
        pltpu.with_memory_space_constraint(array, pltpu.HBM)
        for array in (features, right_side, lengthscale.reshape(1, feats))
    ]
    far_off = pl.BlockSpec(memory_space=pltpu.HBM)
    rows, right, inverse = call(
        row_copies, *given, specs=[far_off] * 3,
        outs=[
            shaped(BF16, plane, feats + probes, width), pltpu.VMEM(block.shape, F32), pltpu.VMEM((feats, width), F32),
        ],
        scratch=[pltpu.VMEM(features.shape, BF16), pltpu.VMEM((1, feats), F32), pltpu.SemaphoreType.DMA((3,)),
                 pltpu.VMEM((feats + probes, width), BF16), pltpu.SemaphoreType.DMA((plane,))],
        out_specs=[far_off, VMEM, VMEM],
    )
    right, inverse = held(right), held(inverse)
    near = exchange(rows, ("x", "z"))
    raw = features[None]
    for axis in COLS[:2]:
        raw = lax.all_gather(raw, axis, axis=0, tiled=True)
    other = lax.ppermute(raw, COLS[2], swap)
    middle = ny // 2 * width
    held_cols = shaped(BF16, middle, feats + EXTRA)
    cols = call(columns, inverse, raw, outs=held_cols)
    near, cols = lax.optimization_barrier((near, cols))
    far = lax.ppermute(near, "core", swap)
    tile = pltpu.VMEM((middle, plane * width), BF16)
    wide = shaped(BF16, feats + EXTRA, plane * width)
    sums = shaped(F32, probes, middle)
    tile_own, sums_near, rows_near = call(own_half, inverse, cols, near, outs=[tile, sums, wide], limit=24)
    tile_own_far, sums_far, rows_far = call(own_half, inverse, cols, far, outs=[tile, sums, wide], limit=24)
    tile_other, tile_other_far, parts = call(
        other_half, inverse, other, near, far, rows_near, rows_far, sums_near, sums_far,
        outs=[tile, tile, shaped(BF16, ny, (ny + 1) * probes, width)],
        limit=24,
        scratch=[pltpu.VMEM((middle, feats + EXTRA), BF16)],
    )
    parts = exchange(parts, COLS)
    image, rows = call(
        functools.partial(spread, factor), parts, outs=[block, shaped(BF16, plane, probes, width)]
    )
    both = lax.all_gather(exchange(rows, ("x", "z")), "core")
    sums = call(
        functools.partial(second_product, factor), held(tile_own), held(tile_own_far), held(tile_other), held(tile_other_far), both, parts, right, image,
        outs=shaped(F32, ny, probes + PAD, width),
    )
    second, local = call(gathered, exchange(sums, COLS), outs=[block, shaped(F32, plane * ncore, width)])
    everyone = exchange(local, ("x", "z", "core"))
    return call(finish, everyone, right, image, second, outs=[block, block])


def solution(mesh):
    fine = Mesh(mesh.devices.reshape(4, 8, 2, 2, 2, 2), AXES)
    split = P(None, AXES)
    return jax.shard_map(
        per_device,
        mesh=fine,
        in_specs=(split, P(), split),
        out_specs=(split, split),
        check_vma=False,
    )
```
